512 devices in a mesh: acct: 128 (over z, x, core), attr: 4 (over y).
Axes of the slice: x: 4, y: 4, z: 16, core: 2. Of those that a mesh axis runs over, the one named last changes fastest.
Arguments:
- scores0: bfloat16 [65536, 128], P('acct'), may hold values from -6 to 6
- seed_mask: int32 [65536], P('acct'), may hold values 0 or 1
- acct_degree: int32 [65536], P('acct'), may hold values from 1 to 16
- attr_degree: int32 [4, 16384], P('attr', 'acct'), may hold values from 1 to 16
- tile_weight: bfloat16 [4, 2048, 128, 128], P('attr', 'acct'), may hold values from -0.125 to 0.125
- tile_acct: int32 [4, 2048], P('attr', 'acct'), may hold values from 0 to 3
- tile_attr: int32 [4, 2048], P('attr', 'acct'), may hold values from 0 to 127
- attr_owner: int32 [4, 128], P('attr'), may hold values from 0 to 127, each once within a row
- tile_count: int32 [4, 128], P('attr', 'acct'), may hold values from 4 to 16, as said below
Outputs:
- new_scores: float32 [65536, 128], P('acct')
- attr_scores: bfloat16 [4, 16384, 128], P('attr', 'acct')
The draws below stay inside these ranges and needn't reach their ends.
Inputs may be any that keep to these rules, and one draw needn't show every extreme that they name: `attr_owner`: each row is a permutation of the attribute blocks' owners. `tile_count`: slots at or past a device's count are unused; in every type some device has all 16 slots live.
All inputs are finite; a program needn't handle non-finite values. No bound on the sum of `seed_mask` on one device may be relied on, other than what follows from the above.
Results may differ from the reference program's by a relative error of at most 0.005.
Values may be sent and summed in bfloat16 or wider, within the bound.
No kernel may reach another device: no remote copies, remote signals or barrier semaphores. Data moves between devices by JAX's collectives and lax.ppermute only.
A program may use at most 64 MiB of HBM per device.

```python
import math
import jax
import jax.numpy as jnp
import numpy as np
from jax import lax

K = 128
TB = 128
TMAX = 16
TYPES = 4
BLOCKS = 128
ACC_BLK = 4
ACCOUNTS = 65536
ATTRS = 16384
TILES = 2048
N_ACCT = 128


def draw_tile_count(key, part):
    key = jax.random.fold_in(key, 11)
    first_key, second_key = jax.random.split(key)
    counts = jax.random.randint(first_key, (TYPES, N_ACCT), TMAX // 4, TMAX + 1)
    full_device = jax.random.randint(second_key, (TYPES, 1), 0, N_ACCT)
    filled = jnp.where(jnp.arange(N_ACCT)[None, :] == full_device, TMAX, counts)
    return filled.astype(jnp.int32)


def set_ends(array, stream_key, least, top_value):
    longest = array.shape.index(max(array.shape))
    spots = []
    for shift in (0, 1):
        where = [jax.random.randint(jax.random.fold_in(stream_key, axis), (), 0, length) for axis, length in enumerate(array.shape)]
        where[longest] = (where[longest] + shift) % array.shape[longest]
        spots.append(tuple(where))
    return array.at[spots[0]].set(least).at[spots[1]].set(top_value)


def shard_levels(own_key, extent, cuts, low, high):
    def one(axis_at, shards_of):
        steps = jax.random.uniform(jax.random.fold_in(jax.random.fold_in(own_key, 6), axis_at), (shards_of,), jnp.float32, low / len(cuts), high / len(cuts))
        return jnp.repeat(jnp.exp(steps), extent[axis_at] // shards_of).reshape((-1,) + (1,) * (len(extent) - axis_at - 1))

    factor_of = one(*cuts[0])
    for cut in cuts[1:]:
        factor_of = factor_of * one(*cut)
    return factor_of


def cumulative_ranks(amount, skew):
    loads = [(1 << 20) // math.isqrt(grade ** skew) + 1 for grade in range(1, amount + 1)]
    deviation = 1 + sum(loads) // (1 << 30)
    return np.cumsum(np.array([max(1, weight // deviation) for weight in loads]))


def ranked(own_key, dims, amount, skew):
    grid = cumulative_ranks(amount, skew)
    pick = jax.random.randint(jax.random.fold_in(own_key, 1), dims, 0, int(grid[amount - 1]))
    rank = jnp.searchsorted(jnp.asarray(grid, jnp.int32), pick, side="right")
    return jax.random.permutation(jax.random.fold_in(own_key, 2), amount)[rank].astype(jnp.int32)


def scatter_about(own_key, dims, spread, reach, shards=(), held_as=jnp.bfloat16):
    loudness = shard_levels(own_key, dims, shards, -0.22, 0.18) if shards else 1.0
    result = jax.random.normal(own_key, dims, jnp.float32) * spread * loudness
    return jnp.minimum(jnp.maximum(result, -reach), reach).astype(held_as)


def setup_inputs(seed: int = 0) -> dict:
    splits = jax.random.split(jax.random.key(seed), 10)
    return {
        "scores0": scatter_about(splits[0], (ACCOUNTS, K), 1.0, 6.0, ((0, 128),)),
        "seed_mask": set_ends((jax.random.randint(splits[1], (ACCOUNTS,), 0, 8) < 1).astype(jnp.int32), jax.random.fold_in(splits[1], 1), 0, 1),
        "acct_degree": set_ends(jax.random.randint(splits[2], (ACCOUNTS,), 1, 17), jax.random.fold_in(splits[2], 1), 1, 16).astype(jnp.int32),
        "attr_degree": set_ends(jax.random.randint(splits[3], (TYPES, ATTRS), 1, 17), jax.random.fold_in(splits[3], 1), 1, 16).astype(jnp.int32),
        "tile_weight": scatter_about(splits[4], (TYPES, TILES, TB, TB), (TB * TMAX) ** -0.5, 0.125, ((0, 4), (1, 128))),
        "tile_acct": set_ends(jax.random.randint(splits[5], (TYPES, TILES), 0, ACC_BLK), jax.random.fold_in(splits[5], 1), 0, ACC_BLK - 1).astype(jnp.int32),
        "tile_attr": set_ends(ranked(splits[6], (TYPES, TILES), BLOCKS, 2), jax.random.fold_in(splits[6], 3), 0, BLOCKS - 1).astype(jnp.int32),
        "attr_owner": jax.vmap(lambda own: jax.random.permutation(own, BLOCKS))(jax.random.split(splits[7], TYPES)).reshape((TYPES, BLOCKS)).astype(jnp.int32),
        "tile_count": draw_tile_count(jax.random.fold_in(splits[9], 71), 0),
    }


ALPHA = 0.8

def reference(scores0, seed_mask, acct_degree, attr_degree, tile_weight, tile_acct, tile_attr, attr_owner, tile_count):
    acct_scale = lax.rsqrt(acct_degree.astype(jnp.float32))
    prior_scores = scores0.astype(jnp.float32)
    scaled = (prior_scores * acct_scale[:, None]).astype(jnp.bfloat16)
    blocks = scaled.reshape(N_ACCT, ACC_BLK, TB, K)
    slot_index = jnp.arange(TMAX)
    returned_sum = jnp.zeros((N_ACCT, ACC_BLK, TB, K), jnp.float32)
    attr_list = []
    for type_index in range(TYPES):
        weights = tile_weight[type_index].reshape(N_ACCT, TMAX, TB, TB)
        acct_ids = tile_acct[type_index].reshape(N_ACCT, TMAX).astype(jnp.int32)
        targets = attr_owner[type_index][tile_attr[type_index]].reshape(N_ACCT, TMAX).astype(jnp.int32)
        living = (slot_index[None, :] < tile_count[type_index][:, None]).astype(jnp.float32)

        def forward(running, pieces):
            weight_fragment, acct_piece, target_piece, live_piece, row_blocks = pieces
            selected_entries = row_blocks[acct_piece].astype(jnp.float32)
            signal_payload = jnp.einsum('und,unq->udq', weight_fragment.astype(jnp.float32), selected_entries)
            signal_payload = signal_payload * live_piece[:, None, None]
            return (running + jax.ops.segment_sum(signal_payload, target_piece, num_segments=N_ACCT), None)
        gathered, unused = lax.scan(forward, jnp.zeros((N_ACCT, TB, K), jnp.float32), (weights, acct_ids, targets, living, blocks))
        attr_scale = lax.rsqrt(attr_degree[type_index].astype(jnp.float32)).reshape(N_ACCT, TB)
        attr_block = (gathered * attr_scale[:, :, None]).astype(jnp.bfloat16)

        def backward(pieces):
            weight_fragment, acct_piece, target_piece, live_piece = pieces
            loaded_values = attr_block[target_piece].astype(jnp.float32)
            reverse_contributions = jnp.einsum('pyb,pbw->pyw', weight_fragment.astype(jnp.float32), loaded_values)
            reverse_contributions = reverse_contributions * live_piece[:, None, None]
            return jax.ops.segment_sum(reverse_contributions, acct_piece, num_segments=ACC_BLK)
        returned_sum = returned_sum + lax.map(backward, (weights, acct_ids, targets, living))
        attr_list.append(attr_block.reshape(ATTRS, K))
    pooled_total = returned_sum.reshape(ACCOUNTS, K) * acct_scale[:, None]
    new_scores = jnp.where(seed_mask[:, None] == 1, prior_scores, ALPHA * pooled_total + (1.0 - ALPHA) * prior_scores)
    return (new_scores, jnp.stack(attr_list))
```

```python
import functools
import jax
import jax.numpy as jnp
from jax import lax
from jax.experimental import pallas as pl
from jax.experimental.pallas import tpu as pltpu
from jax.sharding import Mesh, PartitionSpec as P

ALPHA = 0.8
ACCT = ("zh", "zl", "x", "c")
SIDE = 128
SLOTS = 16
ROWS = 512

AHEAD = [(2 * x + c, 2 * ((x + (1, -1)[c]) % 4) + c) for x in range(4) for c in range(2)]
BACK = [(b, a) for a, b in AHEAD]
SWAP = [(0, 1), (1, 0)]


def place(code, me):
    owner = code & 127
    x = (owner >> 1) & 3
    z = owner >> 3
    away = jnp.where(me[1] == 0, x - me[0], me[0] - x) & 3
    along = (z & 3) * 4 + (z >> 2)
    taken = ((code >> 9) == 1) & ((owner & 1) == me[1])
    return taken, away, along, (code >> 7) & 3


def forward_kernel(me, code0, code1, w0, w1, x0, x1, o0, o1, o2, o3, acc):
    acc[...] = jnp.zeros_like(acc)
    for code, w, rows in ((code0, w0, x0), (code1, w1, x1)):

        def step(s, carry, code=code, w=w, rows=rows):
            taken, away, along, block = place(code[s], me)

            @pl.when(taken)
            def _():
                start = pl.multiple_of(block * SIDE, SIDE)
                acc[away * 16 + along] += lax.dot_general(
                    w[s],
                    rows[pl.ds(start, SIDE), :],
                    (((0,), (0,)), ((), ())),
                    preferred_element_type=jnp.float32,
                )

            return carry

        lax.fori_loop(0, SLOTS, step, 0)
    for n, out in enumerate((o0, o1, o2, o3)):
        out[...] = acc[n * 16 : (n + 1) * 16].astype(out.dtype)


def backward_kernel(me, code0, code1, w0, w1, g0, g1, g2, g3, mine, other, acc):
    acc[...] = jnp.zeros_like(acc)
    for half, (code, w) in enumerate(((code0, w0), (code1, w1))):

        def step(s, carry, half=half, code=code, w=w):
            taken, away, along, block = place(code[s], me)
            for n, blocks in enumerate((g0, g1, g2, g3)):

                @pl.when(taken & (away == n))
                def _(blocks=blocks):
                    start = pl.multiple_of(half * ROWS + block * SIDE, SIDE)
                    acc[pl.ds(start, SIDE), :] += jnp.dot(
                        w[s], blocks[along], preferred_element_type=jnp.float32
                    )

            return carry

        lax.fori_loop(0, SLOTS, step, 0)
    mine[...] = acc[:ROWS]
    other[...] = acc[ROWS:].astype(other.dtype)


def smem(n):
    return [pl.BlockSpec(memory_space=pltpu.SMEM)] * n


def vmem(n):
    return [pl.BlockSpec(memory_space=pltpu.VMEM)] * n


def per_device(
    scores0,
    seed_mask,
    acct_degree,
    attr_degree,
    tile_weight,
    tile_acct,
    tile_attr,
    attr_owner,
    tile_count,
):
    bf16, f32 = jnp.bfloat16, jnp.float32
    weights = tile_weight[0]
    acct_scale = lax.rsqrt(acct_degree.astype(f32))
    prior_scores = scores0.astype(f32)
    scaled = (prior_scores * acct_scale[:, None]).astype(bf16)
    lookup = tile_attr[0][:, None] == jnp.arange(SIDE)[None, :]
    targets = jnp.sum(jnp.where(lookup, attr_owner[0][None, :], 0), axis=1)
    living = (jnp.arange(SLOTS) < tile_count[0, 0]).astype(jnp.int32)
    code = targets + tile_acct[0] * 128 + living * 512
    me = jnp.stack([lax.axis_index("x"), lax.axis_index("c")]).astype(jnp.int32)

    weights1 = lax.ppermute(weights, "c", SWAP)
    code1 = lax.ppermute(code, "c", SWAP)
    scaled1 = lax.ppermute(scaled, "c", SWAP)

    group = jax.ShapeDtypeStruct((16, SIDE, SIDE), bf16)
    o0, o1, o2, o3 = pl.pallas_call(
        forward_kernel,
        out_shape=[group] * 4,
        in_specs=smem(3) + vmem(4),
        out_specs=vmem(4),
        scratch_shapes=[pltpu.VMEM((64, SIDE, SIDE), f32)],
        compiler_params=pltpu.CompilerParams(vmem_limit_bytes=32 * 2**20),
        cost_estimate=pl.CostEstimate(
            flops=2 * 16 * SIDE**3, bytes_accessed=4 * 2**20, transcendentals=0
        ),
    )(me, code, code1, weights, weights1, scaled, scaled1)

    xc = ("x", "c")
    far = lax.ppermute(o2, xc, AHEAD)
    near = lax.ppermute(o3, xc, BACK)
    rest = lax.ppermute((o1.astype(f32) + far.astype(f32)).astype(bf16), xc, AHEAD)
    line = (o0.astype(f32) + near.astype(f32) + rest.astype(f32)).astype(bf16)
    line = line.reshape(4, 4, SIDE, SIDE)
    line = lax.all_to_all(line, "zl", 0, 0, tiled=True)
    quarter = jnp.sum(line.astype(f32), axis=0).astype(bf16)
    quarter = lax.all_to_all(quarter, "zh", 0, 0, tiled=True)
    own_sum = jnp.sum(quarter.astype(f32), axis=0)
    attr_scale = lax.rsqrt(attr_degree[0].astype(f32))
    own_scores = (own_sum * attr_scale[:, None]).astype(bf16)

    spread = jnp.broadcast_to(own_scores[None], (4, SIDE, SIDE))
    spread = lax.all_to_all(spread, "zh", 0, 0, tiled=True)
    spread = jnp.broadcast_to(spread[None], (4, 4, SIDE, SIDE))
    g0 = lax.all_to_all(spread, "zl", 0, 0, tiled=True).reshape(16, SIDE, SIDE)
    g3 = lax.ppermute(g0, xc, AHEAD)
    g1 = lax.ppermute(g0, xc, BACK)
    g2 = lax.ppermute(g3, xc, AHEAD)

    mine, other = pl.pallas_call(
        backward_kernel,
        out_shape=[
            jax.ShapeDtypeStruct((ROWS, SIDE), f32),
            jax.ShapeDtypeStruct((ROWS, SIDE), bf16),
        ],
        in_specs=smem(3) + vmem(6),
        out_specs=vmem(2),
        scratch_shapes=[pltpu.VMEM((2 * ROWS, SIDE), f32)],
        compiler_params=pltpu.CompilerParams(vmem_limit_bytes=32 * 2**20),
        cost_estimate=pl.CostEstimate(
            flops=2 * 16 * SIDE**3, bytes_accessed=4 * 2**20, transcendentals=0
        ),
    )(me, code, code1, weights, weights1, g0, g1, g2, g3)

    returned = (mine + lax.ppermute(other, "c", SWAP).astype(f32)).astype(bf16)
    returned = jnp.broadcast_to(returned[None], (4, ROWS, SIDE))
    returned = lax.all_to_all(returned, "y", 0, 0, tiled=True)
    whole_sum = jnp.sum(returned.astype(f32), axis=0)
    new_scores = jnp.where(
        seed_mask[:, None] == 1,
        prior_scores,
        ALPHA * (whole_sum * acct_scale[:, None]) + (1.0 - ALPHA) * prior_scores,
    )
    return (new_scores, own_scores[None])


def solution(mesh):
    fine = Mesh(mesh.devices.reshape(4, 4, 4, 2, 4), ACCT + ("y",))
    placed = (
        P(ACCT, None),
        P(ACCT),
        P(ACCT),
        P("y", ACCT),
        P("y", ACCT, None, None),
        P("y", ACCT),
        P("y", ACCT),
        P("y", None),
        P("y", ACCT),
    )
    return jax.shard_map(
        per_device,
        mesh=fine,
        in_specs=placed,
        out_specs=(P(ACCT, None), P("y", ACCT, None)),
        check_vma=False,
    )
```

```python
import functools
import jax
import jax.numpy as jnp
from jax import lax
from jax.experimental import pallas as pl
from jax.experimental.pallas import tpu as pltpu
from jax.sharding import Mesh, PartitionSpec as P

ALPHA = 0.8
ACCT = ("z", "x", "c")
SIDE = 128
SLOTS = 16
ROWS = 512
LINE = 16
MEBI = 2**20

AHEAD = [(2 * x + c, 2 * ((x + (1, -1)[c]) % 4) + c) for x in range(4) for c in range(2)]
BACK = [(b, a) for a, b in AHEAD]
SWAP = [(0, 1), (1, 0)]


def place(code, me):
    owner = code & 127
    x = (owner >> 1) & 3
    away = jnp.where(me[1] == 0, x - me[0], me[0] - x) & 3
    taken = ((code >> 9) == 1) & ((owner & 1) == me[1])
    return taken, away, owner >> 3, (code >> 7) & 3


def column(row):
    return jnp.broadcast_to(row, (SIDE, SIDE)).T


def prepare_kernel(table, attr, acct, count, scores, degree, payload, code):
    lane = lax.broadcasted_iota(jnp.int32, (SLOTS, SIDE), 1)
    tail = jnp.zeros((SLOTS, SIDE), jnp.int32)
    for s in range(SLOTS):
        owner = table[0, attr[0, s]]
        placing = acct[0, s] + jnp.where(s < count[0, 0], 4, 0)
        code[s] = owner + placing * 128
        tail = jnp.where(lane == s, owner, tail)
        tail = jnp.where(lane == s + SLOTS, placing, tail)
    payload[ROWS:] = tail.astype(jnp.float32).astype(payload.dtype)
    for n in range(4):
        rows = pl.ds(n * SIDE, SIDE)
        scale = column(lax.rsqrt(degree[n : n + 1, :].astype(jnp.float32)))
        payload[rows, :] = (scores[rows, :].astype(jnp.float32) * scale).astype(payload.dtype)


def finish_kernel(t0, t1, t2, t3, scores, degree, seed, new):
    for n in range(4):
        rows = pl.ds(n * SIDE, SIDE)
        scale = column(lax.rsqrt(degree[n : n + 1, :].astype(jnp.float32)))
        prior = scores[rows, :].astype(jnp.float32)
        f32 = [t[rows, :].astype(jnp.float32) for t in (t0, t1, t2, t3)]
        whole = (f32[0] + f32[2]) + (f32[1] + f32[3])
        mixed = ALPHA * (whole * scale) + (1.0 - ALPHA) * prior
        kept = column(seed[n : n + 1, :].astype(jnp.float32))
        new[rows, :] = jnp.where(kept == 1.0, prior, mixed)


def forward_kernel(offsets, me, code0, code1, w0, w1, x0, x1, *refs):
    outs, acc = refs[:-1], refs[-1]
    acc[...] = jnp.zeros_like(acc)
    for code, w, rows in ((code0, w0, x0), (code1, w1, x1)):

        def step(s, carry, code=code, w=w, rows=rows):
            taken, away, z, block = place(code[s], me)
            index = jnp.int32(0)
            wanted = jnp.bool_(False)
            for n, offset in enumerate(offsets):
                index = jnp.where(away == offset, n * LINE, index)
                wanted = wanted | (away == offset)

            @pl.when(taken & wanted)
            def _():
                start = pl.multiple_of(block * SIDE, SIDE)
                acc[index + z] += lax.dot_general(
                    w[s],
                    rows[pl.ds(start, SIDE), :],
                    (((0,), (0,)), ((), ())),
                    preferred_element_type=jnp.float32,
                )

            return carry

        lax.fori_loop(0, SLOTS, step, 0)
    for n, out in enumerate(outs):
        out[...] = acc[n * LINE : (n + 1) * LINE].astype(out.dtype)


def owner_kernel(parts, degree, own, spread):
    scale = column(lax.rsqrt(degree[...].astype(jnp.float32)))
    total = parts[0].astype(jnp.float32)
    for n in range(1, LINE):
        total += parts[n].astype(jnp.float32)
    scores = (total * scale).astype(own.dtype)
    own[...] = scores
    for n in range(LINE):
        spread[n] = scores


def backward_kernel(me, code0, code1, w0, w1, g0, g1, g2, g3, mine, other, acc):
    acc[...] = jnp.zeros_like(acc)
    for half, (code, w) in enumerate(((code0, w0), (code1, w1))):

        def step(s, carry, half=half, code=code, w=w):
            taken, away, z, block = place(code[s], me)
            for n, blocks in enumerate((g0, g1, g2, g3)):

                @pl.when(taken & (away == n))
                def _(blocks=blocks):
                    start = pl.multiple_of(half * ROWS + block * SIDE, SIDE)
                    acc[pl.ds(start, SIDE), :] += jnp.dot(
                        w[s], blocks[z], preferred_element_type=jnp.float32
                    )

            return carry

        lax.fori_loop(0, SLOTS, step, 0)
    mine[...] = acc[:ROWS]
    other[...] = acc[ROWS:].astype(other.dtype)


def smem(n):
    return [pl.BlockSpec(memory_space=pltpu.SMEM)] * n


def vmem(n):
    return [pl.BlockSpec(memory_space=pltpu.VMEM)] * n


def call(kernel, outs, specs, scratch, flops, moved, out_specs=None):
    return pl.pallas_call(
        kernel,
        out_shape=outs,
        in_specs=specs,
        out_specs=out_specs or vmem(len(outs)),
        scratch_shapes=scratch,
        compiler_params=pltpu.CompilerParams(vmem_limit_bytes=24 * MEBI),
        cost_estimate=pl.CostEstimate(flops=flops, bytes_accessed=moved, transcendentals=0),
    )


def per_device(
    scores0,
    seed_mask,
    acct_degree,
    attr_degree,
    tile_weight,
    tile_acct,
    tile_attr,
    attr_owner,
    tile_count,
):
    bf16, f32, i32 = jnp.bfloat16, jnp.float32, jnp.int32
    group = jax.ShapeDtypeStruct((LINE, SIDE, SIDE), bf16)
    block = jax.ShapeDtypeStruct((SIDE, SIDE), bf16)
    weights = tile_weight[0]
    weights1 = lax.ppermute(weights, "c", SWAP)

    degree = acct_degree.reshape(4, SIDE)
    payload, code = call(
        prepare_kernel,
        [
            jax.ShapeDtypeStruct((ROWS + SLOTS, SIDE), bf16),
            jax.ShapeDtypeStruct((SLOTS,), i32),
        ],
        smem(4) + vmem(2),
        [],
        ROWS * SIDE,
        MEBI // 4,
        vmem(1) + smem(1),
    )(attr_owner, tile_attr, tile_acct, tile_count, scores0, degree)
    payload1 = lax.ppermute(payload, "c", SWAP)
    tail1 = payload1[ROWS].astype(i32)
    code1 = tail1[:SLOTS] + tail1[SLOTS : 2 * SLOTS] * 128
    me = jnp.stack([lax.axis_index("x"), lax.axis_index("c")]).astype(i32)

    tiles = 2 * 10 * SIDE**3
    slots = (me, code, code1, weights, weights1)

    def forward(offsets):
        return call(
            functools.partial(forward_kernel, offsets),
            [group] * len(offsets),
            smem(3) + vmem(4),
            [pltpu.VMEM((len(offsets) * LINE, SIDE, SIDE), f32)],
            tiles,
            3 * MEBI,
        )(*slots, payload, payload1)

    (o2,) = forward((2,))
    far = lax.ppermute(o2, ("x", "c"), AHEAD)
    o3, o1, o0 = forward((3, 1, 0))
    near = lax.ppermute(o3, ("x", "c"), BACK)
    rest = (o1.astype(f32) + far.astype(f32)).astype(bf16)
    rest = lax.ppermute(rest, ("x", "c"), AHEAD)
    line = (o0.astype(f32) + near.astype(f32) + rest.astype(f32)).astype(bf16)
    line = lax.all_to_all(line, "z", 0, 0, tiled=True)
    own_scores, spread = call(
        owner_kernel, [block, group], vmem(2), [], SIDE * SIDE * LINE, MEBI
    )(line, attr_degree)

    g0 = lax.all_to_all(spread, "z", 0, 0, tiled=True)
    g3 = lax.ppermute(g0, ("x", "c"), AHEAD)
    g1 = lax.ppermute(g0, ("x", "c"), BACK)
    g2 = lax.ppermute(g3, ("x", "c"), AHEAD)
    mine, other = call(
        backward_kernel,
        [jax.ShapeDtypeStruct((ROWS, SIDE), f32), jax.ShapeDtypeStruct((ROWS, SIDE), bf16)],
        smem(3) + vmem(6),
        [pltpu.VMEM((2 * ROWS, SIDE), f32)],
        tiles,
        4 * MEBI,
    )(*slots, g0, g1, g2, g3)

    returned = (mine + lax.ppermute(other, "c", SWAP).astype(f32)).astype(bf16)
    types = [returned]
    for shift in (1, 2, 3):
        ring = [(y, (y + shift) % 4) for y in range(4)]
        types.append(lax.ppermute(returned, "y", ring))
    (new_scores,) = call(
        finish_kernel,
        [jax.ShapeDtypeStruct((ROWS, SIDE), f32)],
        vmem(7),
        [],
        ROWS * SIDE * 8,
        MEBI,
    )(*types, scores0, degree, seed_mask.reshape(4, SIDE))
    return (new_scores, own_scores[None])


def solution(mesh):
    fine = Mesh(mesh.devices.reshape(LINE, 4, 2, 4), ACCT + ("y",))
    placed = (
        P(ACCT, None),
        P(ACCT),
        P(ACCT),
        P("y", ACCT),
        P("y", ACCT, None, None),
        P("y", ACCT),
        P("y", ACCT),
        P("y", None),
        P("y", ACCT),
    )
    return jax.shard_map(
        per_device,
        mesh=fine,
        in_specs=placed,
        out_specs=(P(ACCT, None), P("y", ACCT, None)),
        check_vma=False,
    )
```

```python
import functools
import jax
import jax.numpy as jnp
from jax import lax
from jax.experimental import pallas as pl
from jax.experimental.pallas import tpu as pltpu
from jax.sharding import Mesh, PartitionSpec as P

ALPHA = 0.8
ACCT = ("zh", "zl", "x", "c")
SIDE = 128
SLOTS = 16
ROWS = 512
LINE = 16
MEBI = 2**20

SWAP = [(0, 1), (1, 0)]
TILES = SLOTS * SIDE
SENT = TILES + ROWS + SLOTS
FOUR = 4 * SIDE
FIRST = [(2 * h + c, 2 * (3 - h if c else h ^ 1) + c) for h in range(4) for c in range(2)]
SECOND = [(2 * h + c, 2 * (h ^ 1 if c else 3 - h) + c) for h in range(4) for c in range(2)]


def shift(n):
    return [(i, (i + n) % 4) for i in range(4)]


def place(code, me):
    owner = code & 127
    z = owner >> 3
    away = (((owner >> 1) & 3) - me[0]) & 3
    taken = ((code >> 9) == 1) & ((owner & 1) == me[1])
    return taken, away, (z & 3) * 4 + (z >> 2), (code >> 7) & 3


def column(row):
    return jnp.broadcast_to(row, (SIDE, SIDE)).T


def prepare_kernel(table, attr, acct, count, weights, scores, degree, payload, code):
    lane = lax.broadcasted_iota(jnp.int32, (SLOTS, SIDE), 1)
    tail = jnp.zeros((SLOTS, SIDE), jnp.int32)
    for s in range(SLOTS):
        owner = table[0, attr[0, s]]
        placing = acct[0, s] + jnp.where(s < count[0, 0], 4, 0)
        code[s] = owner + placing * 128
        tail = jnp.where(lane == s, owner, tail)
        tail = jnp.where(lane == s + SLOTS, placing, tail)
        payload[s * SIDE : (s + 1) * SIDE, :] = weights[0, s]
    payload[TILES + ROWS :, :] = tail.astype(jnp.float32).astype(payload.dtype)
    for n in range(4):
        rows = pl.ds(n * SIDE, SIDE)
        scale = column(lax.rsqrt(degree[n : n + 1, :].astype(jnp.float32)))
        scaled = scores[rows, :].astype(jnp.float32) * scale
        payload[pl.ds(TILES + n * SIDE, SIDE), :] = scaled.astype(payload.dtype)


def tile(sent, s):
    return sent[pl.ds(pl.multiple_of(s * SIDE, SIDE), SIDE), :]


def forward_kernel(offsets, me, code0, code1, sent0, sent1, *refs):
    outs, acc = refs[:-1], refs[-1]
    acc[...] = jnp.zeros_like(acc)
    for code, sent in ((code0, sent0), (code1, sent1)):

        def step(s, carry, code=code, sent=sent):
            taken, away, along, block = place(code[s], me)
            index = jnp.int32(0)
            wanted = jnp.bool_(False)
            for n, offset in enumerate(offsets):
                index = jnp.where(away == offset, n * LINE, index)
                wanted = wanted | (away == offset)

            @pl.when(taken & wanted)
            def _():
                acc[index + along] += lax.dot_general(
                    tile(sent, s),
                    tile(sent, SLOTS + block),
                    (((0,), (0,)), ((), ())),
                    preferred_element_type=jnp.float32,
                )

            return carry

        lax.fori_loop(0, SLOTS, step, 0)
    for n, out in enumerate(outs):
        out[...] = acc[n * LINE : (n + 1) * LINE].astype(out.dtype)


def near_kernel(me, parts, degree, sums):
    for n in range(4):
        total = parts[0, n].astype(jnp.float32)
        for k in range(1, 4):
            total += parts[k, n].astype(jnp.float32)
        sums[n * SIDE : (n + 1) * SIDE, :] = total.astype(sums.dtype)
    row = lax.broadcasted_iota(jnp.int32, (SLOTS, SIDE), 0)
    mine = jnp.where(row == me[2], degree[...].astype(jnp.float32), 0.0)
    sums[FOUR:, :] = mine.astype(sums.dtype)


def far_kernel(me, mine, other, own, scores):
    degree = mine[FOUR:, :].astype(jnp.float32) + other[FOUR:, :].astype(jnp.float32)
    for n in range(4):
        rows = pl.ds(n * SIDE, SIDE)
        total = mine[rows, :].astype(jnp.float32) + other[rows, :].astype(jnp.float32)
        scale = column(lax.rsqrt(degree[n : n + 1, :]))
        scores[rows, :] = (total * scale).astype(scores.dtype)
    own[...] = scores[pl.ds(pl.multiple_of(me[2] * SIDE, SIDE), SIDE), :]


def backward_kernel(me, code0, code1, sent0, sent1, g0, g1, g2, g3, mine, other, acc):
    acc[...] = jnp.zeros_like(acc)
    for half, (code, sent) in enumerate(((code0, sent0), (code1, sent1))):

        def step(s, carry, half=half, code=code, sent=sent):
            taken, away, along, block = place(code[s], me)
            for n, blocks in enumerate((g0, g1, g2, g3)):

                @pl.when(taken & (away == n))
                def _(blocks=blocks):
                    start = pl.multiple_of(half * ROWS + block * SIDE, SIDE)
                    acc[pl.ds(start, SIDE), :] += jnp.dot(
                        tile(sent, s), tile(blocks, along), preferred_element_type=jnp.float32
                    )

            return carry

        lax.fori_loop(0, SLOTS, step, 0)
    mine[...] = acc[:ROWS]
    other[...] = acc[ROWS:].astype(other.dtype)


def finish_kernel(types, scores, degree, seed, new):
    for n in range(4):
        rows = pl.ds(n * SIDE, SIDE)
        scale = column(lax.rsqrt(degree[n : n + 1, :].astype(jnp.float32)))
        prior = scores[rows, :].astype(jnp.float32)
        whole = types[0, rows, :].astype(jnp.float32)
        for k in range(1, 4):
            whole += types[k, rows, :].astype(jnp.float32)
        mixed = ALPHA * (whole * scale) + (1.0 - ALPHA) * prior
        kept = column(seed[n : n + 1, :].astype(jnp.float32))
        new[rows, :] = jnp.where(kept == 1.0, prior, mixed)


def smem(n):
    return [pl.BlockSpec(memory_space=pltpu.SMEM)] * n


def vmem(n):
    return [pl.BlockSpec(memory_space=pltpu.VMEM)] * n


def call(kernel, outs, specs, scratch, flops, moved, out_specs=None):
    return pl.pallas_call(
        kernel,
        out_shape=outs,
        in_specs=specs,
        out_specs=out_specs or vmem(len(outs)),
        scratch_shapes=scratch,
        compiler_params=pltpu.CompilerParams(vmem_limit_bytes=24 * MEBI),
        cost_estimate=pl.CostEstimate(flops=flops, bytes_accessed=moved, transcendentals=0),
    )


def per_device(
    scores0,
    seed_mask,
    acct_degree,
    attr_degree,
    tile_weight,
    tile_acct,
    tile_attr,
    attr_owner,
    tile_count,
):
    bf16, f32, i32 = jnp.bfloat16, jnp.float32, jnp.int32
    group = jax.ShapeDtypeStruct((LINE, SIDE, SIDE), bf16)
    degree = acct_degree.reshape(4, SIDE)
    payload, code = call(
        prepare_kernel,
        [jax.ShapeDtypeStruct((SENT, SIDE), bf16), jax.ShapeDtypeStruct((SLOTS,), i32)],
        smem(4) + vmem(3),
        [],
        ROWS * SIDE,
        MEBI,
        vmem(1) + smem(1),
    )(attr_owner, tile_attr, tile_acct, tile_count, tile_weight, scores0, degree)
    payload1 = lax.ppermute(payload, "c", SWAP)
    tail1 = payload1[TILES + ROWS].astype(i32)
    code1 = tail1[:SLOTS] + tail1[SLOTS : 2 * SLOTS] * 128
    me = jnp.stack([lax.axis_index(axis) for axis in ("x", "c", "zh")]).astype(i32)

    tiles = 2 * 10 * SIDE**3
    slots = (me, code, code1, payload, payload1)

    def forward(offsets):
        return call(
            functools.partial(forward_kernel, offsets),
            [group] * len(offsets),
            smem(3) + vmem(2),
            [pltpu.VMEM((len(offsets) * LINE, SIDE, SIDE), f32)],
            tiles,
            3 * MEBI,
        )(*slots)

    (o2,) = forward((2,))
    r2 = lax.ppermute(o2, "x", shift(2))
    o1, o3, o0 = forward((1, 3, 0))
    r1 = lax.ppermute(o1, "x", shift(1))
    r3 = lax.ppermute(o3, "x", shift(3))
    line = o0.astype(f32) + r1.astype(f32) + r2.astype(f32) + r3.astype(f32)
    line = line.astype(bf16).reshape(4, 4, SIDE, SIDE)
    line = lax.all_to_all(line, "zl", 0, 0, tiled=True)
    sums = jax.ShapeDtypeStruct((FOUR + SLOTS, SIDE), bf16)
    (near,) = call(
        near_kernel, [sums], smem(1) + vmem(2), [], SIDE * SIDE * LINE, MEBI
    )(me, line, attr_degree)
    half = near.astype(f32) + lax.ppermute(near, ("zh", "c"), FIRST).astype(f32)
    half = half.astype(bf16)
    rest = lax.ppermute(half, ("zh", "c"), SECOND)
    own_scores, scores = call(
        far_kernel,
        [jax.ShapeDtypeStruct((SIDE, SIDE), bf16), jax.ShapeDtypeStruct((FOUR, SIDE), bf16)],
        smem(1) + vmem(2),
        [],
        SIDE * SIDE * LINE,
        MEBI // 2,
    )(me, half, rest)

    g0 = lax.all_gather(scores, "zl", axis=0, tiled=True)
    g2 = lax.ppermute(g0, "x", shift(2))
    g3 = lax.ppermute(g0, "x", shift(1))
    g1 = lax.ppermute(g0, "x", shift(3))
    mine, other = call(
        backward_kernel,
        [jax.ShapeDtypeStruct((ROWS, SIDE), f32), jax.ShapeDtypeStruct((ROWS, SIDE), bf16)],
        smem(3) + vmem(6),
        [pltpu.VMEM((2 * ROWS, SIDE), f32)],
        tiles,
        4 * MEBI,
    )(*slots, g0, g1, g2, g3)

    returned = (mine + lax.ppermute(other, "c", SWAP).astype(f32)).astype(bf16)
    types = jnp.broadcast_to(returned[None], (4, ROWS, SIDE))
    types = lax.all_to_all(types, "y", 0, 0, tiled=True)
    (new_scores,) = call(
        finish_kernel,
        [jax.ShapeDtypeStruct((ROWS, SIDE), f32)],
        vmem(4),
        [],
        ROWS * SIDE * 8,
        MEBI,
    )(types, scores0, degree, seed_mask.reshape(4, SIDE))
    return (new_scores, own_scores[None])


def solution(mesh):
    fine = Mesh(mesh.devices.reshape(4, 4, 4, 2, 4), ACCT + ("y",))
    placed = (
        P(ACCT, None),
        P(ACCT),
        P(ACCT),
        P("y", ACCT),
        P("y", ACCT, None, None),
        P("y", ACCT),
        P("y", ACCT),
        P("y", None),
        P("y", ACCT),
    )
    return jax.shard_map(
        per_device,
        mesh=fine,
        in_specs=placed,
        out_specs=(P(ACCT, None), P("y", ACCT, None)),
        check_vma=False,
    )
```

```python
import functools
import jax
import jax.numpy as jnp
from jax import lax
from jax.experimental import pallas as pl
from jax.experimental.pallas import tpu as pltpu
from jax.sharding import PartitionSpec as P

ALPHA = 0.8
SIDE = 128
SLOTS = 16
ROWS = 512
LINE = 16
MEBI = 2**20
TILES = SLOTS * SIDE
SENT = TILES + ROWS + SLOTS
FOUR = 4 * SIDE


def device(core, u, v):
    return (((u + core) % 16) * 4 + (v + core) % 4) * 2 + core


def pairs(meet):
    return [
        (device(c, u, v), device(c, *meet(c, u, v)))
        for c in range(2)
        for u in range(16)
        for v in range(4)
    ]


SWAP = [(i, i ^ 1) for i in range(128)]
BESIDE = pairs(lambda c, u, v: (u ^ 1, v))
ACROSS = pairs(lambda c, u, v: (u, v ^ 1))
DIAGONAL = pairs(lambda c, u, v: (u ^ 1, v ^ 1))
FIRST = pairs(lambda c, u, v: (u ^ 4 if c == 0 else 12 - (u & 12) + (u & 3), v))
SECOND = pairs(lambda c, u, v: (u ^ 4 if c == 1 else 12 - (u & 12) + (u & 3), v))
QUADS = [
    [device(c, far * 4 + step * 2 + odd, (0, 3, 1, 2)[side * 2 + end]) for end in (0, 1) for step in (0, 1)]
    for c in (0, 1)
    for side in (0, 1)
    for odd in (0, 1)
    for far in range(4)
]


def where(index):
    core = index & 1
    return core, ((index >> 3) - core) & 15, ((index >> 1) - core) & 3


def place(code, me):
    core, u, v = where(me[0])
    core1, u1, v1 = where(code & 127)
    side = (v ^ (v >> 1) ^ v1 ^ (v1 >> 1)) & 1
    taken = ((code >> 9) == 1) & (core1 == core)
    along = (v1 >> 1) * 8 + ((u1 >> 1) & 1) * 4 + (u1 >> 2)
    return taken, side * 2 + ((u ^ u1) & 1), along, (code >> 7) & 3


def column(row):
    return jnp.broadcast_to(row, (SIDE, SIDE)).T


def prepare_kernel(table, attr, acct, count, weights, scores, degree, payload, code, rows, sems):
    tiles = pltpu.make_async_copy(weights, payload.at[pl.ds(0, TILES), :], sems.at[0])
    prior = pltpu.make_async_copy(scores, rows, sems.at[1])
    prior.start()
    tiles.start()
    lane = lax.broadcasted_iota(jnp.int32, (SLOTS, SIDE), 1)
    tail = jnp.zeros((SLOTS, SIDE), jnp.int32)
    for s in range(SLOTS):
        owner = table[0, attr[0, s]]
        placing = acct[0, s] + jnp.where(s < count[0, 0], 4, 0)
        code[s] = owner + placing * 128
        tail = jnp.where(lane == s, owner, tail)
        tail = jnp.where(lane == s + SLOTS, placing, tail)
    payload[TILES + ROWS :, :] = tail.astype(jnp.float32).astype(payload.dtype)
    prior.wait()
    for n in range(4):
        scale = column(lax.rsqrt(degree[n : n + 1, :].astype(jnp.float32)))
        scaled = rows[pl.ds(n * SIDE, SIDE), :].astype(jnp.float32) * scale
        payload[pl.ds(TILES + n * SIDE, SIDE), :] = scaled.astype(payload.dtype)
    tiles.wait()


def tile(sent, s):
    return sent[pl.ds(pl.multiple_of(s * SIDE, SIDE), SIDE), :]


def forward_kernel(offsets, me, code0, code1, sent0, sent1, *refs):
    outs, acc = refs[:-1], refs[-1]
    acc[...] = jnp.zeros_like(acc)
    for code, sent in ((code0, sent0), (code1, sent1)):

        def step(s, carry, code=code, sent=sent):
            taken, away, along, block = place(code[s], me)
            index = jnp.int32(0)
            wanted = jnp.bool_(False)
            for n, offset in enumerate(offsets):
                index = jnp.where(away == offset, n * LINE, index)
                wanted = wanted | (away == offset)

            @pl.when(taken & wanted)
            def _():
                acc[index + along] += lax.dot_general(
                    tile(sent, s),
                    tile(sent, SLOTS + block),
                    (((0,), (0,)), ((), ())),
                    preferred_element_type=jnp.float32,
                )

            return carry

        lax.fori_loop(0, SLOTS, step, 0)
    for n, out in enumerate(outs):
        out[...] = acc[n * LINE : (n + 1) * LINE].astype(out.dtype)


def near_kernel(me, parts, degree, sums):
    for n in range(4):
        total = parts[0, n].astype(jnp.float32)
        for k in range(1, 4):
            total += parts[k, n].astype(jnp.float32)
        sums[n * SIDE : (n + 1) * SIDE, :] = total.astype(sums.dtype)
    row = lax.broadcasted_iota(jnp.int32, (SLOTS, SIDE), 0)
    mine = jnp.where(row == where(me[0])[1] >> 2, degree[...].astype(jnp.float32), 0.0)
    sums[FOUR:, :] = mine.astype(sums.dtype)


def far_kernel(me, mine, other, own, spread):
    degree = mine[FOUR:, :].astype(jnp.float32) + other[FOUR:, :].astype(jnp.float32)
    for n in range(4):
        rows = pl.ds(n * SIDE, SIDE)
        total = mine[rows, :].astype(jnp.float32) + other[rows, :].astype(jnp.float32)
        scores = (total * column(lax.rsqrt(degree[n : n + 1, :]))).astype(spread.dtype)
        for k in range(4):
            spread[k, rows, :] = scores
    far = where(me[0])[1] >> 2
    own[...] = spread[0, pl.ds(pl.multiple_of(far * SIDE, SIDE), SIDE), :]


def backward_kernel(chips, me, code0, code1, sent0, sent1, *refs):
    groups, refs = refs[: len(chips)], refs[len(chips) :]
    if len(refs) == 1:
        (acc,) = refs
        acc[...] = jnp.zeros_like(acc)
    else:
        before, mine, other, acc = refs
        acc[...] = before[...]
    for half, (code, sent) in enumerate(((code0, sent0), (code1, sent1))):

        def step(s, carry, half=half, code=code, sent=sent):
            taken, chip, along, block = place(code[s], me)
            for n, blocks in zip(chips, groups):

                @pl.when(taken & (chip == n))
                def _(blocks=blocks):
                    start = pl.multiple_of(half * ROWS + block * SIDE, SIDE)
                    acc[pl.ds(start, SIDE), :] += jnp.dot(
                        tile(sent, s), tile(blocks, along), preferred_element_type=jnp.float32
                    )

            return carry

        lax.fori_loop(0, SLOTS, step, 0)
    if len(refs) > 1:
        mine[...] = acc[:ROWS]
        other[...] = acc[ROWS:].astype(other.dtype)


def finish_kernel(types, scores, degree, seed, new):
    for n in range(4):
        rows = pl.ds(n * SIDE, SIDE)
        scale = column(lax.rsqrt(degree[n : n + 1, :].astype(jnp.float32)))
        prior = scores[rows, :].astype(jnp.float32)
        whole = types[0, rows, :].astype(jnp.float32)
        for k in range(1, 4):
            whole += types[k, rows, :].astype(jnp.float32)
        mixed = ALPHA * (whole * scale) + (1.0 - ALPHA) * prior
        kept = column(seed[n : n + 1, :].astype(jnp.float32))
        new[rows, :] = jnp.where(kept == 1.0, prior, mixed)


def smem(n):
    return [pl.BlockSpec(memory_space=pltpu.SMEM)] * n


def vmem(n):
    return [pl.BlockSpec(memory_space=pltpu.VMEM)] * n


def call(kernel, outs, specs, scratch, flops, moved, out_specs=None):
    return pl.pallas_call(
        kernel,
        out_shape=outs,
        in_specs=specs,
        out_specs=out_specs or vmem(len(outs)),
        scratch_shapes=scratch,
        compiler_params=pltpu.CompilerParams(vmem_limit_bytes=24 * MEBI),
        cost_estimate=pl.CostEstimate(flops=flops, bytes_accessed=moved, transcendentals=0),
    )


def per_device(
    scores0,
    seed_mask,
    acct_degree,
    attr_degree,
    tile_weight,
    tile_acct,
    tile_attr,
    attr_owner,
    tile_count,
):
    bf16, f32, i32 = jnp.bfloat16, jnp.float32, jnp.int32
    group = jax.ShapeDtypeStruct((LINE, SIDE, SIDE), bf16)
    degree = acct_degree.reshape(4, SIDE)
    payload, code = call(
        prepare_kernel,
        [jax.ShapeDtypeStruct((SENT, SIDE), bf16), jax.ShapeDtypeStruct((SLOTS,), i32)],
        smem(4) + [pl.BlockSpec(memory_space=pl.ANY)] * 2 + vmem(1),
        [pltpu.VMEM((ROWS, SIDE), bf16), pltpu.SemaphoreType.DMA((2,))],
        ROWS * SIDE,
        MEBI,
        vmem(1) + smem(1),
    )(
        attr_owner,
        tile_attr,
        tile_acct,
        tile_count,
        tile_weight.reshape(TILES, SIDE),
        scores0,
        degree,
    )
    payload1 = lax.ppermute(payload, "acct", SWAP)
    tail1 = payload1[TILES + ROWS].astype(i32)
    code1 = tail1[:SLOTS] + tail1[SLOTS : 2 * SLOTS] * 128
    me = lax.axis_index("acct").astype(i32).reshape(1)

    flops = 2 * 10 * SIDE**3
    slots = (me, code, code1, payload, payload1)

    def forward(chips):
        return call(
            functools.partial(forward_kernel, chips),
            [group] * len(chips),
            smem(3) + vmem(2),
            [pltpu.VMEM((len(chips) * LINE, SIDE, SIDE), f32)],
            flops,
            3 * MEBI,
        )(*slots)

    (o3,) = forward((3,))
    r3 = lax.ppermute(o3, "acct", DIAGONAL)
    o1, o2, o0 = forward((1, 2, 0))
    r1 = lax.ppermute(o1, "acct", BESIDE)
    r2 = lax.ppermute(o2, "acct", ACROSS)
    line = o0.astype(f32) + r1.astype(f32) + r2.astype(f32) + r3.astype(f32)
    line = line.astype(bf16).reshape(4, 4, SIDE, SIDE)
    line = lax.all_to_all(line, "acct", 0, 0, tiled=True, axis_index_groups=QUADS)
    sums = jax.ShapeDtypeStruct((FOUR + SLOTS, SIDE), bf16)
    (near,) = call(
        near_kernel, [sums], smem(1) + vmem(2), [], SIDE * SIDE * LINE, MEBI
    )(me, line, attr_degree)
    half = near.astype(f32) + lax.ppermute(near, "acct", FIRST).astype(f32)
    half = half.astype(bf16)
    rest = lax.ppermute(half, "acct", SECOND)
    own_scores, spread = call(
        far_kernel,
        [
            jax.ShapeDtypeStruct((SIDE, SIDE), bf16),
            jax.ShapeDtypeStruct((4, FOUR, SIDE), bf16),
        ],
        smem(1) + vmem(2),
        [],
        SIDE * SIDE * LINE,
        MEBI // 2,
    )(me, half, rest)

    g0 = lax.all_to_all(spread, "acct", 0, 0, tiled=True, axis_index_groups=QUADS)
    g0 = g0.reshape(LINE * SIDE, SIDE)
    g3 = lax.ppermute(g0, "acct", DIAGONAL)
    g1 = lax.ppermute(g0, "acct", BESIDE)
    g2 = lax.ppermute(g0, "acct", ACROSS)
    acc = jax.ShapeDtypeStruct((2 * ROWS, SIDE), f32)
    (before,) = call(
        functools.partial(backward_kernel, (0,)), [acc], smem(3) + vmem(3), [], flops, 4 * MEBI
    )(*slots, g0)
    mine, other = call(
        functools.partial(backward_kernel, (1, 2, 3)),
        [jax.ShapeDtypeStruct((ROWS, SIDE), f32), jax.ShapeDtypeStruct((ROWS, SIDE), bf16)],
        smem(3) + vmem(6),
        [pltpu.VMEM(acc.shape, f32)],
        flops,
        4 * MEBI,
    )(*slots, g1, g2, g3, before)

    returned = (mine + lax.ppermute(other, "acct", SWAP).astype(f32)).astype(bf16)
    types = jnp.broadcast_to(returned[None], (4, ROWS, SIDE))
    types = lax.all_to_all(types, "attr", 0, 0, tiled=True)
    (new_scores,) = call(
        finish_kernel,
        [jax.ShapeDtypeStruct((ROWS, SIDE), f32)],
        vmem(4),
        [],
        ROWS * SIDE * 8,
        MEBI,
    )(types, scores0, degree, seed_mask.reshape(4, SIDE))
    return (new_scores, own_scores[None])


def solution(mesh):
    placed = (
        P("acct", None),
        P("acct"),
        P("acct"),
        P("attr", "acct"),
        P("attr", "acct", None, None),
        P("attr", "acct"),
        P("attr", "acct"),
        P("attr", None),
        P("attr", "acct"),
    )
    return jax.shard_map(
        per_device,
        mesh=mesh,
        in_specs=placed,
        out_specs=(P("acct", None), P("attr", "acct", None)),
        check_vma=False,
    )
```

```python
import functools
import jax
import jax.numpy as jnp
from jax import lax
from jax.experimental import pallas as pl
from jax.experimental.pallas import tpu as pltpu
from jax.sharding import PartitionSpec as P

ALPHA = 0.8
SIDE = 128
SLOTS = 16
ROWS = 512
LINE = 16
MEBI = 2**20
TILES = SLOTS * SIDE
SENT = TILES + ROWS + SLOTS
FOUR = 4 * SIDE


def device(core, u, v):
    return (((u + core) % 16) * 4 + (v + core) % 4) * 2 + core


def pairs(meet):
    return [
        (device(c, u, v), device(c, *meet(c, u, v)))
        for c in range(2)
        for u in range(16)
        for v in range(4)
    ]


SWAP = [(i, i ^ 1) for i in range(128)]
BESIDE = pairs(lambda c, u, v: (u ^ 1, v))
ACROSS = pairs(lambda c, u, v: (u, v ^ 1))
DIAGONAL = pairs(lambda c, u, v: (u ^ 1, v ^ 1))
FIRST = pairs(lambda c, u, v: (u ^ 4 if c == 0 else 12 - (u & 12) + (u & 3), v))
SECOND = pairs(lambda c, u, v: (u ^ 4 if c == 1 else 12 - (u & 12) + (u & 3), v))
QUADS = [
    [device(c, far * 4 + step * 2 + odd, (0, 3, 1, 2)[side * 2 + end]) for end in (0, 1) for step in (0, 1)]
    for c in (0, 1)
    for side in (0, 1)
    for odd in (0, 1)
    for far in range(4)
]


def where(index):
    core = index & 1
    return core, ((index >> 3) - core) & 15, ((index >> 1) - core) & 3


def decode(owner, core, u, v):
    core1, u1, v1 = where(owner)
    side = (v ^ (v >> 1) ^ v1 ^ (v1 >> 1)) & 1
    chip = jnp.where(core1 == core, side * 2 + ((u ^ u1) & 1), 7)
    return chip * 16 + (v1 >> 1) * 8 + ((u1 >> 1) & 1) * 4 + (u1 >> 2)


def column(row):
    return jnp.broadcast_to(row, (SIDE, SIDE)).T


def prepare_kernel(me, table, attr, acct, count, weights, scores, degree, payload, rows, sems):
    tiles = pltpu.make_async_copy(weights, payload.at[pl.ds(0, TILES), :], sems.at[0])
    prior = pltpu.make_async_copy(scores, rows, sems.at[1])
    prior.start()
    tiles.start()
    core, u, v = where(me[0])
    twin, twin_u, twin_v = where(me[0] ^ 1)
    lane = lax.broadcasted_iota(jnp.int32, (SLOTS, SIDE), 1)
    tail = jnp.zeros((SLOTS, SIDE), jnp.int32)
    for s in range(SLOTS):
        owner = table[0, attr[0, s]]
        live = s < count[0, 0]
        tail = jnp.where(lane == s, jnp.where(live, decode(owner, core, u, v), 112), tail)
        sent = jnp.where(live, decode(owner, twin, twin_u, twin_v), 112)
        tail = jnp.where(lane == s + SLOTS, sent, tail)
        tail = jnp.where(lane == s + 2 * SLOTS, acct[0, s], tail)
    payload[TILES + ROWS :, :] = tail.astype(jnp.float32).astype(payload.dtype)
    prior.wait()
    for n in range(4):
        scale = column(lax.rsqrt(degree[n : n + 1, :].astype(jnp.float32)))
        scaled = rows[pl.ds(n * SIDE, SIDE), :].astype(jnp.float32) * scale
        payload[pl.ds(TILES + n * SIDE, SIDE), :] = scaled.astype(payload.dtype)
    tiles.wait()


def tile(sent, s):
    return sent[pl.ds(pl.multiple_of(s * SIDE, SIDE), SIDE), :]


def forward_kernel(offsets, tail0, tail1, sent0, sent1, *refs):
    outs, acc = refs[:-1], refs[-1]
    acc[...] = jnp.zeros_like(acc)
    for half, (tail, sent) in enumerate(((tail0, sent0), (tail1, sent1))):

        def step(s, carry, half=half, tail=tail, sent=sent):
            code, block = tail[0, half * SLOTS + s], tail[0, 2 * SLOTS + s]
            chip, along = code >> 4, code & 15
            index = jnp.int32(0)
            wanted = jnp.bool_(False)
            for n, offset in enumerate(offsets):
                index = jnp.where(chip == offset, n * LINE, index)
                wanted = wanted | (chip == offset)

            @pl.when(wanted)
            def _():
                acc[index + along] += lax.dot_general(
                    tile(sent, s),
                    tile(sent, SLOTS + block),
                    (((0,), (0,)), ((), ())),
                    preferred_element_type=jnp.float32,
                )

            return carry

        lax.fori_loop(0, SLOTS, step, 0)
    for n, out in enumerate(outs):
        out[...] = acc[n * LINE : (n + 1) * LINE].astype(out.dtype)


def near_kernel(me, parts, degree, sums):
    for n in range(4):
        total = parts[0, n].astype(jnp.float32)
        for k in range(1, 4):
            total += parts[k, n].astype(jnp.float32)
        sums[n * SIDE : (n + 1) * SIDE, :] = total.astype(sums.dtype)
    row = lax.broadcasted_iota(jnp.int32, (SLOTS, SIDE), 0)
    mine = jnp.where(row == where(me[0])[1] >> 2, degree[...].astype(jnp.float32), 0.0)
    sums[FOUR:, :] = mine.astype(sums.dtype)


def far_kernel(me, mine, other, own, spread):
    degree = mine[FOUR:, :].astype(jnp.float32) + other[FOUR:, :].astype(jnp.float32)
    for n in range(4):
        rows = pl.ds(n * SIDE, SIDE)
        total = mine[rows, :].astype(jnp.float32) + other[rows, :].astype(jnp.float32)
        scores = (total * column(lax.rsqrt(degree[n : n + 1, :]))).astype(spread.dtype)
        for k in range(4):
            spread[k, rows, :] = scores
    far = where(me[0])[1] >> 2
    own[...] = spread[0, pl.ds(pl.multiple_of(far * SIDE, SIDE), SIDE), :]


def backward_kernel(chips, tail0, tail1, sent0, sent1, *refs):
    groups, refs = refs[: len(chips)], refs[len(chips) :]
    if len(refs) == 1:
        (acc,) = refs
        acc[...] = jnp.zeros_like(acc)
    else:
        before, mine, other, acc = refs
        acc[...] = before[...]
    for half, (tail, sent) in enumerate(((tail0, sent0), (tail1, sent1))):

        def step(s, carry, half=half, tail=tail, sent=sent):
            code, block = tail[0, half * SLOTS + s], tail[0, 2 * SLOTS + s]
            chip, along = code >> 4, code & 15
            for n, blocks in zip(chips, groups):

                @pl.when(chip == n)
                def _(blocks=blocks):
                    start = pl.multiple_of(half * ROWS + block * SIDE, SIDE)
                    acc[pl.ds(start, SIDE), :] += jnp.dot(
                        tile(sent, s), tile(blocks, along), preferred_element_type=jnp.float32
                    )

            return carry

        lax.fori_loop(0, SLOTS, step, 0)
    if len(refs) > 1:
        mine[...] = acc[:ROWS]
        other[...] = acc[ROWS:].astype(other.dtype)


def finish_kernel(types, scores, degree, seed, new):
    for n in range(4):
        rows = pl.ds(n * SIDE, SIDE)
        scale = column(lax.rsqrt(degree[n : n + 1, :].astype(jnp.float32)))
        prior = scores[rows, :].astype(jnp.float32)
        whole = types[0, rows, :].astype(jnp.float32)
        for k in range(1, 4):
            whole += types[k, rows, :].astype(jnp.float32)
        mixed = ALPHA * (whole * scale) + (1.0 - ALPHA) * prior
        kept = column(seed[n : n + 1, :].astype(jnp.float32))
        new[rows, :] = jnp.where(kept == 1.0, prior, mixed)


def smem(n):
    return [pl.BlockSpec(memory_space=pltpu.SMEM)] * n


def vmem(n):
    return [pl.BlockSpec(memory_space=pltpu.VMEM)] * n


def call(kernel, outs, specs, scratch, flops, moved):
    return pl.pallas_call(
        kernel,
        out_shape=outs,
        in_specs=specs,
        out_specs=vmem(len(outs)),
        scratch_shapes=scratch,
        compiler_params=pltpu.CompilerParams(vmem_limit_bytes=24 * MEBI),
        cost_estimate=pl.CostEstimate(flops=flops, bytes_accessed=moved, transcendentals=0),
    )


def per_device(
    scores0,
    seed_mask,
    acct_degree,
    attr_degree,
    tile_weight,
    tile_acct,
    tile_attr,
    attr_owner,
    tile_count,
):
    bf16, f32, i32 = jnp.bfloat16, jnp.float32, jnp.int32
    group = jax.ShapeDtypeStruct((LINE, SIDE, SIDE), bf16)
    degree = acct_degree.reshape(4, SIDE)
    me = lax.axis_index("acct").astype(i32).reshape(1)
    (payload,) = call(
        prepare_kernel,
        [jax.ShapeDtypeStruct((SENT, SIDE), bf16)],
        smem(5) + [pl.BlockSpec(memory_space=pltpu.HBM)] * 2 + vmem(1),
        [pltpu.VMEM((ROWS, SIDE), bf16), pltpu.SemaphoreType.DMA((2,))],
        ROWS * SIDE,
        MEBI,
    )(
        me,
        attr_owner,
        tile_attr,
        tile_acct,
        tile_count,
        pltpu.with_memory_space_constraint(tile_weight.reshape(TILES, SIDE), pltpu.HBM),
        pltpu.with_memory_space_constraint(scores0, pltpu.HBM),
        degree,
    )
    payload1 = lax.ppermute(payload, "acct", SWAP)
    flops = 2 * 10 * SIDE**3
    tails = [sent[TILES + ROWS :][:1].astype(i32) for sent in (payload, payload1)]
    slots = (*tails, payload, payload1)

    def forward(chips):
        return call(
            functools.partial(forward_kernel, chips),
            [group] * len(chips),
            smem(2) + vmem(2),
            [pltpu.VMEM((len(chips) * LINE, SIDE, SIDE), f32)],
            flops,
            3 * MEBI,
        )(*slots)

    (o3,) = forward((3,))
    r3 = lax.ppermute(o3, "acct", DIAGONAL)
    o1, o2 = forward((1, 2))
    r1 = lax.ppermute(o1, "acct", BESIDE)
    r2 = lax.ppermute(o2, "acct", ACROSS)
    (o0,) = forward((0,))
    line = o0.astype(f32) + r1.astype(f32) + r2.astype(f32) + r3.astype(f32)
    line = line.astype(bf16).reshape(4, 4, SIDE, SIDE)
    line = lax.all_to_all(line, "acct", 0, 0, tiled=True, axis_index_groups=QUADS)
    sums = jax.ShapeDtypeStruct((FOUR + SLOTS, SIDE), bf16)
    (near,) = call(
        near_kernel, [sums], smem(1) + vmem(2), [], SIDE * SIDE * LINE, MEBI
    )(me, line, attr_degree)
    half = near.astype(f32) + lax.ppermute(near, "acct", FIRST).astype(f32)
    half = half.astype(bf16)
    rest = lax.ppermute(half, "acct", SECOND)
    own_scores, spread = call(
        far_kernel,
        [
            jax.ShapeDtypeStruct((SIDE, SIDE), bf16),
            jax.ShapeDtypeStruct((4, FOUR, SIDE), bf16),
        ],
        smem(1) + vmem(2),
        [],
        SIDE * SIDE * LINE,
        MEBI // 2,
    )(me, half, rest)

    g0 = lax.all_to_all(spread, "acct", 0, 0, tiled=True, axis_index_groups=QUADS)
    g0 = g0.reshape(LINE * SIDE, SIDE)
    g3 = lax.ppermute(g0, "acct", DIAGONAL)
    g1 = lax.ppermute(g0, "acct", BESIDE)
    g2 = lax.ppermute(g0, "acct", ACROSS)
    acc = jax.ShapeDtypeStruct((2 * ROWS, SIDE), f32)
    (before,) = call(
        functools.partial(backward_kernel, (0,)), [acc], smem(2) + vmem(3), [], flops, 4 * MEBI
    )(*slots, g0)
    mine, other = call(
        functools.partial(backward_kernel, (1, 2, 3)),
        [jax.ShapeDtypeStruct((ROWS, SIDE), f32), jax.ShapeDtypeStruct((ROWS, SIDE), bf16)],
        smem(2) + vmem(6),
        [pltpu.VMEM(acc.shape, f32)],
        flops,
        4 * MEBI,
    )(*slots, g1, g2, g3, before)

    returned = (mine + lax.ppermute(other, "acct", SWAP).astype(f32)).astype(bf16)
    types = jnp.broadcast_to(returned[None], (4, ROWS, SIDE))
    types = lax.all_to_all(types, "attr", 0, 0, tiled=True)
    (new_scores,) = call(
        finish_kernel,
        [jax.ShapeDtypeStruct((ROWS, SIDE), f32)],
        vmem(4),
        [],
        ROWS * SIDE * 8,
        MEBI,
    )(types, scores0, degree, seed_mask.reshape(4, SIDE))
    return (new_scores, own_scores[None])


def solution(mesh):
    placed = (
        P("acct", None),
        P("acct"),
        P("acct"),
        P("attr", "acct"),
        P("attr", "acct", None, None),
        P("attr", "acct"),
        P("attr", "acct"),
        P("attr", None),
        P("attr", "acct"),
    )
    return jax.shard_map(
        per_device,
        mesh=mesh,
        in_specs=placed,
        out_specs=(P("acct", None), P("attr", "acct", None)),
        check_vma=False,
    )
```

```python
import functools
import jax
import jax.numpy as jnp
from jax import lax
from jax.experimental import pallas as pl
from jax.experimental.pallas import tpu as pltpu
from jax.sharding import PartitionSpec as P

ALPHA = 0.8
SIDE = 128
SLOTS = 16
ROWS = 512
LINE = 16
MEBI = 2**20
TILES = SLOTS * SIDE
SENT = TILES + ROWS + SLOTS
FOUR = 4 * SIDE


def device(core, u, v):
    return (((u + core) % 16) * 4 + (v + core) % 4) * 2 + core


def pairs(meet):
    return [
        (device(c, u, v), device(c, *meet(c, u, v)))
        for c in range(2)
        for u in range(16)
        for v in range(4)
    ]


SWAP = [(i, i ^ 1) for i in range(128)]
BESIDE = pairs(lambda c, u, v: (u ^ 1, v))
ACROSS = pairs(lambda c, u, v: (u, v ^ 1))
DIAGONAL = pairs(lambda c, u, v: (u ^ 1, v ^ 1))
QUADS = [
    [device(c, far * 4 + step * 2 + odd, (0, 3, 1, 2)[side * 2 + end]) for end in (0, 1) for step in (0, 1)]
    for c in (0, 1)
    for side in (0, 1)
    for odd in (0, 1)
    for far in range(4)
]
FARS = [
    [device(c, far * 4 + step, v) for far in range(4)]
    for c in (0, 1)
    for step in range(4)
    for v in range(4)
]


def where(index):
    core = index & 1
    return core, ((index >> 3) - core) & 15, ((index >> 1) - core) & 3


def decode(owner, core, u, v):
    core1, u1, v1 = where(owner)
    side = (v ^ (v >> 1) ^ v1 ^ (v1 >> 1)) & 1
    chip = jnp.where(core1 == core, side * 2 + ((u ^ u1) & 1), 7)
    return chip * 16 + (v1 >> 1) * 8 + ((u1 >> 1) & 1) * 4 + (u1 >> 2)


def column(row):
    return jnp.broadcast_to(row, (SIDE, SIDE)).T


def prepare_kernel(me, table, attr, acct, count, weights, scores, degree, payload, rows, sems):
    tiles = pltpu.make_async_copy(weights, payload.at[pl.ds(0, TILES), :], sems.at[0])
    prior = pltpu.make_async_copy(scores, rows, sems.at[1])
    prior.start()
    tiles.start()
    core, u, v = where(me[0])
    twin, twin_u, twin_v = where(me[0] ^ 1)
    lane = lax.broadcasted_iota(jnp.int32, (SLOTS, SIDE), 1)
    tail = jnp.zeros((SLOTS, SIDE), jnp.int32)
    for s in range(SLOTS):
        owner = table[0, attr[0, s]]
        live = s < count[0, 0]
        tail = jnp.where(lane == s, jnp.where(live, decode(owner, core, u, v), 112), tail)
        sent = jnp.where(live, decode(owner, twin, twin_u, twin_v), 112)
        tail = jnp.where(lane == s + SLOTS, sent, tail)
        tail = jnp.where(lane == s + 2 * SLOTS, acct[0, s], tail)
    payload[TILES + ROWS :, :] = tail.astype(jnp.float32).astype(payload.dtype)
    prior.wait()
    for n in range(4):
        scale = column(lax.rsqrt(degree[n : n + 1, :].astype(jnp.float32)))
        scaled = rows[pl.ds(n * SIDE, SIDE), :].astype(jnp.float32) * scale
        payload[pl.ds(TILES + n * SIDE, SIDE), :] = scaled.astype(payload.dtype)
    tiles.wait()


def tile(sent, s):
    return sent[pl.ds(pl.multiple_of(s * SIDE, SIDE), SIDE), :]


def forward_kernel(offsets, tail0, tail1, sent0, sent1, *refs):
    outs, acc = refs[:-1], refs[-1]
    acc[...] = jnp.zeros_like(acc)
    for half, (tail, sent) in enumerate(((tail0, sent0), (tail1, sent1))):

        def step(s, carry, half=half, tail=tail, sent=sent):
            code, block = tail[0, half * SLOTS + s], tail[0, 2 * SLOTS + s]
            chip, along = code >> 4, code & 15
            index = jnp.int32(0)
            wanted = jnp.bool_(False)
            for n, offset in enumerate(offsets):
                index = jnp.where(chip == offset, n * LINE, index)
                wanted = wanted | (chip == offset)

            @pl.when(wanted)
            def _():
                acc[index + along] += lax.dot_general(
                    tile(sent, s),
                    tile(sent, SLOTS + block),
                    (((0,), (0,)), ((), ())),
                    preferred_element_type=jnp.float32,
                )

            return carry

        lax.fori_loop(0, SLOTS, step, 0)
    for n, out in enumerate(outs):
        out[...] = acc[n * LINE : (n + 1) * LINE].astype(out.dtype)


def near_kernel(parts, degree, sums):
    for n in range(4):
        total = parts[0, n].astype(jnp.float32)
        for k in range(1, 4):
            total += parts[k, n].astype(jnp.float32)
        sums[n * SIDE : (n + 1) * SIDE, :] = total.astype(sums.dtype)
    sums[FOUR:, :] = jnp.broadcast_to(degree[...].astype(jnp.float32), (SLOTS, SIDE)).astype(sums.dtype)


def far_kernel(me, parts, own, spread):
    for n in range(4):
        rows = pl.ds(n * SIDE, SIDE)
        total = parts[0, rows, :].astype(jnp.float32)
        for k in range(1, 4):
            total += parts[k, rows, :].astype(jnp.float32)
        degree = parts[n, FOUR:, :].astype(jnp.float32)[:1]
        scores = (total * column(lax.rsqrt(degree))).astype(spread.dtype)
        for k in range(4):
            spread[k, rows, :] = scores
    far = where(me[0])[1] >> 2
    own[...] = spread[0, pl.ds(pl.multiple_of(far * SIDE, SIDE), SIDE), :]


def backward_kernel(chips, tail0, tail1, sent0, sent1, *refs):
    groups, refs = refs[: len(chips)], refs[len(chips) :]
    if len(refs) == 1:
        (acc,) = refs
        acc[...] = jnp.zeros_like(acc)
    else:
        before, mine, other, acc = refs
        acc[...] = before[...]
    for half, (tail, sent) in enumerate(((tail0, sent0), (tail1, sent1))):

        def step(s, carry, half=half, tail=tail, sent=sent):
            code, block = tail[0, half * SLOTS + s], tail[0, 2 * SLOTS + s]
            chip, along = code >> 4, code & 15
            for n, blocks in zip(chips, groups):

                @pl.when(chip == n)
                def _(blocks=blocks):
                    start = pl.multiple_of(half * ROWS + block * SIDE, SIDE)
                    acc[pl.ds(start, SIDE), :] += jnp.dot(
                        tile(sent, s), tile(blocks, along), preferred_element_type=jnp.float32
                    )

            return carry

        lax.fori_loop(0, SLOTS, step, 0)
    if len(refs) > 1:
        mine[...] = acc[:ROWS]
        other[...] = acc[ROWS:].astype(other.dtype)


def finish_kernel(types, scores, degree, seed, new):
    for n in range(4):
        rows = pl.ds(n * SIDE, SIDE)
        scale = column(lax.rsqrt(degree[n : n + 1, :].astype(jnp.float32)))
        prior = scores[rows, :].astype(jnp.float32)
        whole = types[0, rows, :].astype(jnp.float32)
        for k in range(1, 4):
            whole += types[k, rows, :].astype(jnp.float32)
        mixed = ALPHA * (whole * scale) + (1.0 - ALPHA) * prior
        kept = column(seed[n : n + 1, :].astype(jnp.float32))
        new[rows, :] = jnp.where(kept == 1.0, prior, mixed)


def smem(n):
    return [pl.BlockSpec(memory_space=pltpu.SMEM)] * n


def vmem(n):
    return [pl.BlockSpec(memory_space=pltpu.VMEM)] * n


def call(kernel, outs, specs, scratch, flops, moved):
    return pl.pallas_call(
        kernel,
        out_shape=outs,
        in_specs=specs,
        out_specs=vmem(len(outs)),
        scratch_shapes=scratch,
        compiler_params=pltpu.CompilerParams(vmem_limit_bytes=24 * MEBI),
        cost_estimate=pl.CostEstimate(flops=flops, bytes_accessed=moved, transcendentals=0),
    )


def per_device(
    scores0,
    seed_mask,
    acct_degree,
    attr_degree,
    tile_weight,
    tile_acct,
    tile_attr,
    attr_owner,
    tile_count,
):
    bf16, f32, i32 = jnp.bfloat16, jnp.float32, jnp.int32
    group = jax.ShapeDtypeStruct((LINE, SIDE, SIDE), bf16)
    degree = acct_degree.reshape(4, SIDE)
    me = lax.axis_index("acct").astype(i32).reshape(1)
    (payload,) = call(
        prepare_kernel,
        [jax.ShapeDtypeStruct((SENT, SIDE), bf16)],
        smem(5) + [pl.BlockSpec(memory_space=pltpu.HBM)] * 2 + vmem(1),
        [pltpu.VMEM((ROWS, SIDE), bf16), pltpu.SemaphoreType.DMA((2,))],
        ROWS * SIDE,
        MEBI,
    )(
        me,
        attr_owner,
        tile_attr,
        tile_acct,
        tile_count,
        pltpu.with_memory_space_constraint(tile_weight.reshape(TILES, SIDE), pltpu.HBM),
        pltpu.with_memory_space_constraint(scores0, pltpu.HBM),
        degree,
    )
    payload1 = lax.ppermute(payload, "acct", SWAP)
    flops = 2 * 10 * SIDE**3
    tails = [sent[TILES + ROWS :][:1].astype(i32) for sent in (payload, payload1)]
    slots = (*tails, payload, payload1)

    def forward(chips):
        return call(
            functools.partial(forward_kernel, chips),
            [group] * len(chips),
            smem(2) + vmem(2),
            [pltpu.VMEM((len(chips) * LINE, SIDE, SIDE), f32)],
            flops,
            3 * MEBI,
        )(*slots)

    (o3,) = forward((3,))
    r3 = lax.ppermute(o3, "acct", DIAGONAL)
    o1, o2 = forward((1, 2))
    r1 = lax.ppermute(o1, "acct", BESIDE)
    r2 = lax.ppermute(o2, "acct", ACROSS)
    (o0,) = forward((0,))
    line = o0.astype(f32) + r1.astype(f32) + r2.astype(f32) + r3.astype(f32)
    line = line.astype(bf16).reshape(4, 4, SIDE, SIDE)
    line = lax.all_to_all(line, "acct", 0, 0, tiled=True, axis_index_groups=QUADS)
    sums = jax.ShapeDtypeStruct((FOUR + SLOTS, SIDE), bf16)
    (near,) = call(near_kernel, [sums], vmem(2), [], SIDE * SIDE * LINE, MEBI)(line, attr_degree)
    fars = lax.all_gather(near, "acct", axis=0, tiled=False, axis_index_groups=FARS)
    own_scores, spread = call(
        far_kernel,
        [
            jax.ShapeDtypeStruct((SIDE, SIDE), bf16),
            jax.ShapeDtypeStruct((4, FOUR, SIDE), bf16),
        ],
        smem(1) + vmem(1),
        [],
        SIDE * SIDE * LINE,
        MEBI // 2,
    )(me, fars)

    g0 = lax.all_to_all(spread, "acct", 0, 0, tiled=True, axis_index_groups=QUADS)
    g0 = g0.reshape(LINE * SIDE, SIDE)
    g3 = lax.ppermute(g0, "acct", DIAGONAL)
    g1 = lax.ppermute(g0, "acct", BESIDE)
    g2 = lax.ppermute(g0, "acct", ACROSS)
    acc = jax.ShapeDtypeStruct((2 * ROWS, SIDE), f32)
    (before,) = call(
        functools.partial(backward_kernel, (0,)), [acc], smem(2) + vmem(3), [], flops, 4 * MEBI
    )(*slots, g0)
    mine, other = call(
        functools.partial(backward_kernel, (3, 1, 2)),
        [jax.ShapeDtypeStruct((ROWS, SIDE), f32), jax.ShapeDtypeStruct((ROWS, SIDE), bf16)],
        smem(2) + vmem(6),
        [pltpu.VMEM(acc.shape, f32)],
        flops,
        4 * MEBI,
    )(*slots, g3, g1, g2, before)

    returned = (mine + lax.ppermute(other, "acct", SWAP).astype(f32)).astype(bf16)
    types = jnp.broadcast_to(returned[None], (4, ROWS, SIDE))
    types = lax.all_to_all(types, "attr", 0, 0, tiled=True)
    (new_scores,) = call(
        finish_kernel,
        [jax.ShapeDtypeStruct((ROWS, SIDE), f32)],
        vmem(4),
        [],
        ROWS * SIDE * 8,
        MEBI,
    )(types, scores0, degree, seed_mask.reshape(4, SIDE))
    return (new_scores, own_scores[None])


def solution(mesh):
    placed = (
        P("acct", None),
        P("acct"),
        P("acct"),
        P("attr", "acct"),
        P("attr", "acct", None, None),
        P("attr", "acct"),
        P("attr", "acct"),
        P("attr", None),
        P("attr", "acct"),
    )
    return jax.shard_map(
        per_device,
        mesh=mesh,
        in_specs=placed,
        out_specs=(P("acct", None), P("attr", "acct", None)),
        check_vma=False,
    )
```

```python
import functools
import jax
import jax.numpy as jnp
from jax import lax
from jax.experimental import pallas as pl
from jax.experimental.pallas import tpu as pltpu
from jax.sharding import PartitionSpec as P

ALPHA = 0.8
SIDE = 128
SLOTS = 16
ROWS = 512
LINE = 16
MEBI = 2**20
TILES = SLOTS * SIDE
SENT = TILES + ROWS + SLOTS
FOUR = 4 * SIDE


def device(core, u, v):
    return (((u + core) % 16) * 4 + (v + core) % 4) * 2 + core


def pairs(meet):
    return [
        (device(c, u, v), device(c, *meet(c, u, v)))
        for c in range(2)
        for u in range(16)
        for v in range(4)
    ]


SWAP = [(i, i ^ 1) for i in range(128)]
BESIDE = pairs(lambda c, u, v: (u ^ 1, v))
ACROSS = pairs(lambda c, u, v: (u, v ^ 1))
DIAGONAL = pairs(lambda c, u, v: (u ^ 1, v ^ 1))
FIRST = pairs(lambda c, u, v: (u ^ 4 if c == 0 else 12 - (u & 12) + (u & 3), v))
SECOND = pairs(lambda c, u, v: (u ^ 4 if c == 1 else 12 - (u & 12) + (u & 3), v))
QUADS = [
    [device(c, far * 4 + step * 2 + odd, (0, 3, 1, 2)[side * 2 + end]) for end in (0, 1) for step in (0, 1)]
    for c in (0, 1)
    for side in (0, 1)
    for odd in (0, 1)
    for far in range(4)
]
def where(index):
    core = index & 1
    return core, ((index >> 3) - core) & 15, ((index >> 1) - core) & 3


def decode(owner, core, u, v):
    core1, u1, v1 = where(owner)
    side = (v ^ (v >> 1) ^ v1 ^ (v1 >> 1)) & 1
    chip = jnp.where(core1 == core, side * 2 + ((u ^ u1) & 1), 7)
    return chip * 16 + (v1 >> 1) * 8 + ((u1 >> 1) & 1) * 4 + (u1 >> 2)


def column(row):
    return jnp.broadcast_to(row, (SIDE, SIDE)).T


def prepare_kernel(me, table, attr, acct, count, weights, scores, degrees, payload, rows, degree, sems):
    tiles = pltpu.make_async_copy(weights, payload.at[pl.ds(0, TILES), :], sems.at[0])
    prior = pltpu.make_async_copy(scores, rows, sems.at[1])
    small = pltpu.make_async_copy(degrees, degree, sems.at[2])
    small.start()
    prior.start()
    tiles.start()
    core, u, v = where(me[0])
    twin, twin_u, twin_v = where(me[0] ^ 1)
    lane = lax.broadcasted_iota(jnp.int32, (SLOTS, SIDE), 1)
    tail = jnp.zeros((SLOTS, SIDE), jnp.int32)
    for s in range(SLOTS):
        owner = table[0, attr[0, s]]
        live = s < count[0, 0]
        tail = jnp.where(lane == s, jnp.where(live, decode(owner, core, u, v), 112), tail)
        sent = jnp.where(live, decode(owner, twin, twin_u, twin_v), 112)
        tail = jnp.where(lane == s + SLOTS, sent, tail)
        tail = jnp.where(lane == s + 2 * SLOTS, acct[0, s], tail)
    payload[TILES + ROWS :, :] = tail.astype(jnp.float32).astype(payload.dtype)
    small.wait()
    prior.wait()
    for n in range(4):
        scale = column(lax.rsqrt(degree[n : n + 1, :].astype(jnp.float32)))
        scaled = rows[pl.ds(n * SIDE, SIDE), :].astype(jnp.float32) * scale
        payload[pl.ds(TILES + n * SIDE, SIDE), :] = scaled.astype(payload.dtype)
    tiles.wait()


def tile(sent, s):
    return sent[pl.ds(pl.multiple_of(s * SIDE, SIDE), SIDE), :]


def forward_kernel(offsets, tail0, tail1, sent0, sent1, *refs):
    outs, acc = refs[:-1], refs[-1]
    acc[...] = jnp.zeros_like(acc)
    for half, (tail, sent) in enumerate(((tail0, sent0), (tail1, sent1))):

        def step(s, carry, half=half, tail=tail, sent=sent):
            code, block = tail[0, half * SLOTS + s], tail[0, 2 * SLOTS + s]
            chip, along = code >> 4, code & 15
            index = jnp.int32(0)
            wanted = jnp.bool_(False)
            for n, offset in enumerate(offsets):
                index = jnp.where(chip == offset, n * LINE, index)
                wanted = wanted | (chip == offset)

            @pl.when(wanted)
            def _():
                acc[index + along] += lax.dot_general(
                    tile(sent, s),
                    tile(sent, SLOTS + block),
                    (((0,), (0,)), ((), ())),
                    preferred_element_type=jnp.float32,
                )

            return carry

        lax.fori_loop(0, SLOTS, step, 0)
    for n, out in enumerate(outs):
        out[...] = acc[n * LINE : (n + 1) * LINE].astype(out.dtype)


def near_kernel(me, parts, degree, sums):
    for n in range(4):
        total = parts[0, n].astype(jnp.float32)
        for k in range(1, 4):
            total += parts[k, n].astype(jnp.float32)
        sums[n * SIDE : (n + 1) * SIDE, :] = total.astype(sums.dtype)
    row = lax.broadcasted_iota(jnp.int32, (SLOTS, SIDE), 0)
    mine = jnp.where(row == where(me[0])[1] >> 2, degree[...].astype(jnp.float32), 0.0)
    sums[FOUR:, :] = mine.astype(sums.dtype)


def far_kernel(me, mine, other, own, spread):
    degree = mine[FOUR:, :].astype(jnp.float32) + other[FOUR:, :].astype(jnp.float32)
    for n in range(4):
        rows = pl.ds(n * SIDE, SIDE)
        total = mine[rows, :].astype(jnp.float32) + other[rows, :].astype(jnp.float32)
        scores = (total * column(lax.rsqrt(degree[n : n + 1, :]))).astype(spread.dtype)
        for k in range(4):
            spread[k, rows, :] = scores
    far = where(me[0])[1] >> 2
    own[...] = spread[0, pl.ds(pl.multiple_of(far * SIDE, SIDE), SIDE), :]


def backward_kernel(chips, halves, *refs):
    tails, sents, refs = refs[: len(halves)], refs[len(halves) : 2 * len(halves)], refs[2 * len(halves) :]
    groups, refs = refs[: len(chips)], refs[len(chips) :]
    if len(refs) == 1:
        (acc,) = refs
        acc[...] = jnp.zeros_like(acc)
        base = 0
    else:
        before, out, acc = refs
        base = halves[0] * ROWS
        acc[...] = before[base : base + ROWS, :]
    for half, tail, sent in zip(halves, tails, sents):

        def step(s, carry, half=half, tail=tail, sent=sent):
            code, block = tail[0, half * SLOTS + s], tail[0, 2 * SLOTS + s]
            chip, along = code >> 4, code & 15
            for n, blocks in zip(chips, groups):

                @pl.when(chip == n)
                def _(blocks=blocks):
                    start = pl.multiple_of(half * ROWS - base + block * SIDE, SIDE)
                    acc[pl.ds(start, SIDE), :] += jnp.dot(
                        tile(sent, s), tile(blocks, along), preferred_element_type=jnp.float32
                    )

            return carry

        lax.fori_loop(0, SLOTS, step, 0)
    if len(refs) > 1:
        out[...] = acc[...].astype(out.dtype)


def finish_kernel(types, scores, degree, seed, new):
    for n in range(4):
        rows = pl.ds(n * SIDE, SIDE)
        scale = column(lax.rsqrt(degree[n : n + 1, :].astype(jnp.float32)))
        prior = scores[rows, :].astype(jnp.float32)
        whole = types[0, rows, :].astype(jnp.float32)
        for k in range(1, 4):
            whole += types[k, rows, :].astype(jnp.float32)
        mixed = ALPHA * (whole * scale) + (1.0 - ALPHA) * prior
        kept = column(seed[n : n + 1, :].astype(jnp.float32))
        new[rows, :] = jnp.where(kept == 1.0, prior, mixed)


def smem(n):
    return [pl.BlockSpec(memory_space=pltpu.SMEM)] * n


def vmem(n):
    return [pl.BlockSpec(memory_space=pltpu.VMEM)] * n


def call(kernel, outs, specs, scratch, flops, moved):
    return pl.pallas_call(
        kernel,
        out_shape=outs,
        in_specs=specs,
        out_specs=vmem(len(outs)),
        scratch_shapes=scratch,
        compiler_params=pltpu.CompilerParams(vmem_limit_bytes=24 * MEBI),
        cost_estimate=pl.CostEstimate(flops=flops, bytes_accessed=moved, transcendentals=0),
    )


def per_device(
    scores0,
    seed_mask,
    acct_degree,
    attr_degree,
    tile_weight,
    tile_acct,
    tile_attr,
    attr_owner,
    tile_count,
):
    bf16, f32, i32 = jnp.bfloat16, jnp.float32, jnp.int32
    group = jax.ShapeDtypeStruct((LINE, SIDE, SIDE), bf16)
    degree = acct_degree.reshape(4, SIDE)
    me = lax.axis_index("acct").astype(i32).reshape(1)
    (payload,) = call(
        prepare_kernel,
        [jax.ShapeDtypeStruct((SENT, SIDE), bf16)],
        smem(5) + [pl.BlockSpec(memory_space=pltpu.HBM)] * 3,
        [
            pltpu.VMEM((ROWS, SIDE), bf16),
            pltpu.VMEM((4, SIDE), i32),
            pltpu.SemaphoreType.DMA((3,)),
        ],
        ROWS * SIDE,
        MEBI,
    )(
        me,
        attr_owner,
        tile_attr,
        tile_acct,
        tile_count,
        *(
            pltpu.with_memory_space_constraint(array, pltpu.HBM)
            for array in (tile_weight.reshape(TILES, SIDE), scores0, degree)
        ),
    )
    payload1 = lax.ppermute(payload, "acct", SWAP)
    flops = 2 * 10 * SIDE**3
    tails = [sent[TILES + ROWS :][:1].astype(i32) for sent in (payload, payload1)]
    slots = (*tails, payload, payload1)

    def forward(chips):
        return call(
            functools.partial(forward_kernel, chips),
            [group] * len(chips),
            smem(2) + vmem(2),
            [pltpu.VMEM((len(chips) * LINE, SIDE, SIDE), f32)],
            flops,
            3 * MEBI,
        )(*slots)

    (o3,) = forward((3,))
    r3 = lax.ppermute(o3, "acct", DIAGONAL)
    o1, o2 = forward((1, 2))
    r1 = lax.ppermute(o1, "acct", BESIDE)
    r2 = lax.ppermute(o2, "acct", ACROSS)
    (o0,) = forward((0,))
    line = o0.astype(f32) + r1.astype(f32) + r2.astype(f32) + r3.astype(f32)
    line = line.astype(bf16).reshape(4, 4, SIDE, SIDE)
    line = lax.all_to_all(line, "acct", 0, 0, tiled=True, axis_index_groups=QUADS)
    sums = jax.ShapeDtypeStruct((FOUR + SLOTS, SIDE), bf16)
    (near,) = call(
        near_kernel, [sums], smem(1) + vmem(2), [], SIDE * SIDE * LINE, MEBI
    )(me, line, attr_degree)
    half = near.astype(f32) + lax.ppermute(near, "acct", FIRST).astype(f32)
    half = half.astype(bf16)
    rest = lax.ppermute(half, "acct", SECOND)
    own_scores, spread = call(
        far_kernel,
        [
            jax.ShapeDtypeStruct((SIDE, SIDE), bf16),
            jax.ShapeDtypeStruct((4, FOUR, SIDE), bf16),
        ],
        smem(1) + vmem(2),
        [],
        SIDE * SIDE * LINE,
        MEBI // 2,
    )(me, half, rest)

    g0 = lax.all_to_all(spread, "acct", 0, 0, tiled=True, axis_index_groups=QUADS)
    g0 = g0.reshape(LINE * SIDE, SIDE)
    g3 = lax.ppermute(g0, "acct", DIAGONAL)
    g1 = lax.ppermute(g0, "acct", BESIDE)
    g2 = lax.ppermute(g0, "acct", ACROSS)
    acc = jax.ShapeDtypeStruct((2 * ROWS, SIDE), f32)
    (before,) = call(
        functools.partial(backward_kernel, (0,), (0, 1)),
        [acc],
        smem(2) + vmem(3),
        [],
        flops,
        4 * MEBI,
    )(*slots, g0)

    def backward(half, dtype):
        (out,) = call(
            functools.partial(backward_kernel, (3, 1, 2), (half,)),
            [jax.ShapeDtypeStruct((ROWS, SIDE), dtype)],
            smem(1) + vmem(5),
            [pltpu.VMEM((ROWS, SIDE), f32)],
            flops,
            2 * MEBI,
        )(slots[half], slots[2 + half], g3, g1, g2, before)
        return out

    other = lax.ppermute(backward(1, bf16), "acct", SWAP)
    returned = (backward(0, f32) + other.astype(f32)).astype(bf16)
    types = jnp.broadcast_to(returned[None], (4, ROWS, SIDE))
    types = lax.all_to_all(types, "attr", 0, 0, tiled=True)
    (new_scores,) = call(
        finish_kernel,
        [jax.ShapeDtypeStruct((ROWS, SIDE), f32)],
        vmem(4),
        [],
        ROWS * SIDE * 8,
        MEBI,
    )(types, scores0, degree, seed_mask.reshape(4, SIDE))
    return (new_scores, own_scores[None])


def solution(mesh):
    placed = (
        P("acct", None),
        P("acct"),
        P("acct"),
        P("attr", "acct"),
        P("attr", "acct", None, None),
        P("attr", "acct"),
        P("attr", "acct"),
        P("attr", None),
        P("attr", "acct"),
    )
    return jax.shard_map(
        per_device,
        mesh=mesh,
        in_specs=placed,
        out_specs=(P("acct", None), P("attr", "acct", None)),
        check_vma=False,
    )
```

```python
import functools
import jax
import jax.numpy as jnp
from jax import lax
from jax.experimental import pallas as pl
from jax.experimental.pallas import tpu as pltpu
from jax.sharding import PartitionSpec as P

ALPHA = 0.8
SIDE = 128
SLOTS = 16
ROWS = 512
LINE = 16
MEBI = 2**20
TILES = SLOTS * SIDE
SENT = TILES + ROWS + SLOTS
FOUR = 4 * SIDE


def device(core, u, v):
    return (((u + core) % 16) * 4 + (v + core) % 4) * 2 + core


def pairs(meet):
    return [
        (device(c, u, v), device(c, *meet(c, u, v)))
        for c in range(2)
        for u in range(16)
        for v in range(4)
    ]


SWAP = [(i, i ^ 1) for i in range(128)]
BESIDE = pairs(lambda c, u, v: (u ^ 1, v))
ACROSS = pairs(lambda c, u, v: (u, v ^ 1))
DIAGONAL = pairs(lambda c, u, v: (u ^ 1, v ^ 1))
FIRST = pairs(lambda c, u, v: (u ^ 4 if c == 0 else 12 - (u & 12) + (u & 3), v))
SECOND = pairs(lambda c, u, v: (u ^ 4 if c == 1 else 12 - (u & 12) + (u & 3), v))
QUADS = [
    [device(c, far * 4 + step * 2 + odd, (0, 3, 1, 2)[side * 2 + end]) for end in (0, 1) for step in (0, 1)]
    for c in (0, 1)
    for side in (0, 1)
    for odd in (0, 1)
    for far in range(4)
]
def where(index):
    core = index & 1
    return core, ((index >> 3) - core) & 15, ((index >> 1) - core) & 3


def decode(owner, core, u, v):
    core1, u1, v1 = where(owner)
    side = (v ^ (v >> 1) ^ v1 ^ (v1 >> 1)) & 1
    chip = jnp.where(core1 == core, side * 2 + ((u ^ u1) & 1), 7)
    return chip * 16 + (v1 >> 1) * 8 + ((u1 >> 1) & 1) * 4 + (u1 >> 2)


def column(row):
    return jnp.broadcast_to(row, (SIDE, SIDE)).T


def prepare_kernel(me, table, attr, acct, count, weights, scores, degrees, payload, rows, degree, sems):
    tiles = pltpu.make_async_copy(weights, payload.at[pl.ds(0, TILES), :], sems.at[0])
    prior = pltpu.make_async_copy(scores, rows, sems.at[1])
    small = pltpu.make_async_copy(degrees, degree, sems.at[2])
    small.start()
    prior.start()
    tiles.start()
    core, u, v = where(me[0])
    twin, twin_u, twin_v = where(me[0] ^ 1)
    lane = lax.broadcasted_iota(jnp.int32, (SLOTS, SIDE), 1)
    tail = jnp.zeros((SLOTS, SIDE), jnp.int32)
    for s in range(SLOTS):
        owner = table[0, attr[0, s]]
        live = s < count[0, 0]
        tail = jnp.where(lane == s, jnp.where(live, decode(owner, core, u, v), 112), tail)
        sent = jnp.where(live, decode(owner, twin, twin_u, twin_v), 112)
        tail = jnp.where(lane == s + SLOTS, sent, tail)
        tail = jnp.where(lane == s + 2 * SLOTS, acct[0, s], tail)
    payload[TILES + ROWS :, :] = tail.astype(jnp.float32).astype(payload.dtype)
    small.wait()
    prior.wait()
    for n in range(4):
        scale = column(lax.rsqrt(degree[n : n + 1, :].astype(jnp.float32)))
        scaled = rows[pl.ds(n * SIDE, SIDE), :].astype(jnp.float32) * scale
        payload[pl.ds(TILES + n * SIDE, SIDE), :] = scaled.astype(payload.dtype)
    tiles.wait()


def tile(sent, s):
    return sent[pl.ds(pl.multiple_of(s * SIDE, SIDE), SIDE), :]


def forward_kernel(offsets, tail0, tail1, sent0, sent1, *refs):
    outs, acc = refs[:-1], refs[-1]
    acc[...] = jnp.zeros_like(acc)
    for half, (tail, sent) in enumerate(((tail0, sent0), (tail1, sent1))):

        def step(s, carry, half=half, tail=tail, sent=sent):
            code, block = tail[0, half * SLOTS + s], tail[0, 2 * SLOTS + s]
            chip, along = code >> 4, code & 15
            index = jnp.int32(0)
            wanted = jnp.bool_(False)
            for n, offset in enumerate(offsets):
                index = jnp.where(chip == offset, n * LINE, index)
                wanted = wanted | (chip == offset)

            @pl.when(wanted)
            def _():
                acc[index + along] += lax.dot_general(
                    tile(sent, s),
                    tile(sent, SLOTS + block),
                    (((0,), (0,)), ((), ())),
                    preferred_element_type=jnp.float32,
                )

            return carry

        lax.fori_loop(0, SLOTS, step, 0, unroll=True)
    for n, out in enumerate(outs):
        out[...] = acc[n * LINE : (n + 1) * LINE].astype(out.dtype)


def near_kernel(me, parts, degree, sums):
    for n in range(4):
        total = parts[0, n].astype(jnp.float32)
        for k in range(1, 4):
            total += parts[k, n].astype(jnp.float32)
        sums[n * SIDE : (n + 1) * SIDE, :] = total.astype(sums.dtype)
    row = lax.broadcasted_iota(jnp.int32, (SLOTS, SIDE), 0)
    mine = jnp.where(row == where(me[0])[1] >> 2, degree[...].astype(jnp.float32), 0.0)
    sums[FOUR:, :] = mine.astype(sums.dtype)


def far_kernel(me, mine, other, own, spread):
    degree = mine[FOUR:, :].astype(jnp.float32) + other[FOUR:, :].astype(jnp.float32)
    for n in range(4):
        rows = pl.ds(n * SIDE, SIDE)
        total = mine[rows, :].astype(jnp.float32) + other[rows, :].astype(jnp.float32)
        scores = (total * column(lax.rsqrt(degree[n : n + 1, :]))).astype(spread.dtype)
        for k in range(4):
            spread[k, rows, :] = scores
    far = where(me[0])[1] >> 2
    own[...] = spread[0, pl.ds(pl.multiple_of(far * SIDE, SIDE), SIDE), :]


def backward_kernel(chips, halves, *refs):
    tails, sents, refs = refs[: len(halves)], refs[len(halves) : 2 * len(halves)], refs[2 * len(halves) :]
    groups, refs = refs[: len(chips)], refs[len(chips) :]
    if len(refs) == 1:
        (acc,) = refs
        acc[...] = jnp.zeros_like(acc)
        base = 0
    else:
        before, out, acc = refs
        base = halves[0] * ROWS
        acc[...] = before[base : base + ROWS, :]
    for half, tail, sent in zip(halves, tails, sents):

        def step(s, carry, half=half, tail=tail, sent=sent):
            code, block = tail[0, half * SLOTS + s], tail[0, 2 * SLOTS + s]
            chip, along = code >> 4, code & 15
            for n, blocks in zip(chips, groups):

                @pl.when(chip == n)
                def _(blocks=blocks):
                    start = pl.multiple_of(half * ROWS - base + block * SIDE, SIDE)
                    acc[pl.ds(start, SIDE), :] += jnp.dot(
                        tile(sent, s), tile(blocks, along), preferred_element_type=jnp.float32
                    )

            return carry

        lax.fori_loop(0, SLOTS, step, 0, unroll=True)
    if len(refs) > 1:
        out[...] = acc[...].astype(out.dtype)


def finish_kernel(types, scores, degree, seed, new):
    for n in range(4):
        rows = pl.ds(n * SIDE, SIDE)
        scale = column(lax.rsqrt(degree[n : n + 1, :].astype(jnp.float32)))
        prior = scores[rows, :].astype(jnp.float32)
        whole = types[0, rows, :].astype(jnp.float32)
        for k in range(1, 4):
            whole += types[k, rows, :].astype(jnp.float32)
        mixed = ALPHA * (whole * scale) + (1.0 - ALPHA) * prior
        kept = column(seed[n : n + 1, :].astype(jnp.float32))
        new[rows, :] = jnp.where(kept == 1.0, prior, mixed)


def smem(n):
    return [pl.BlockSpec(memory_space=pltpu.SMEM)] * n


def vmem(n):
    return [pl.BlockSpec(memory_space=pltpu.VMEM)] * n


def call(kernel, outs, specs, scratch, flops, moved):
    return pl.pallas_call(
        kernel,
        out_shape=outs,
        in_specs=specs,
        out_specs=vmem(len(outs)),
        scratch_shapes=scratch,
        compiler_params=pltpu.CompilerParams(vmem_limit_bytes=24 * MEBI),
        cost_estimate=pl.CostEstimate(flops=flops, bytes_accessed=moved, transcendentals=0),
    )


def per_device(
    scores0,
    seed_mask,
    acct_degree,
    attr_degree,
    tile_weight,
    tile_acct,
    tile_attr,
    attr_owner,
    tile_count,
):
    bf16, f32, i32 = jnp.bfloat16, jnp.float32, jnp.int32
    group = jax.ShapeDtypeStruct((LINE, SIDE, SIDE), bf16)
    degree = acct_degree.reshape(4, SIDE)
    me = lax.axis_index("acct").astype(i32).reshape(1)
    (payload,) = call(
        prepare_kernel,
        [jax.ShapeDtypeStruct((SENT, SIDE), bf16)],
        smem(5) + [pl.BlockSpec(memory_space=pltpu.HBM)] * 3,
        [
            pltpu.VMEM((ROWS, SIDE), bf16),
            pltpu.VMEM((4, SIDE), i32),
            pltpu.SemaphoreType.DMA((3,)),
        ],
        ROWS * SIDE,
        MEBI,
    )(
        me,
        attr_owner,
        tile_attr,
        tile_acct,
        tile_count,
        *(
            pltpu.with_memory_space_constraint(array, pltpu.HBM)
            for array in (tile_weight.reshape(TILES, SIDE), scores0, degree)
        ),
    )
    payload1 = lax.ppermute(payload, "acct", SWAP)
    flops = 2 * 10 * SIDE**3
    tails = [sent[TILES + ROWS :][:1].astype(i32) for sent in (payload, payload1)]
    slots = (*tails, payload, payload1)

    def forward(chips):
        return call(
            functools.partial(forward_kernel, chips),
            [group] * len(chips),
            smem(2) + vmem(2),
            [pltpu.VMEM((len(chips) * LINE, SIDE, SIDE), f32)],
            flops,
            3 * MEBI,
        )(*slots)

    o3, o1, o2 = forward((3, 1, 2))
    r3 = lax.ppermute(o3, "acct", DIAGONAL)
    r1 = lax.ppermute(o1, "acct", BESIDE)
    r2 = lax.ppermute(o2, "acct", ACROSS)
    (o0,) = forward((0,))
    line = o0.astype(f32) + r1.astype(f32) + r2.astype(f32) + r3.astype(f32)
    line = line.astype(bf16).reshape(4, 4, SIDE, SIDE)
    line = lax.all_to_all(line, "acct", 0, 0, tiled=True, axis_index_groups=QUADS)
    sums = jax.ShapeDtypeStruct((FOUR + SLOTS, SIDE), bf16)
    (near,) = call(
        near_kernel, [sums], smem(1) + vmem(2), [], SIDE * SIDE * LINE, MEBI
    )(me, line, attr_degree)
    half = near.astype(f32) + lax.ppermute(near, "acct", FIRST).astype(f32)
    half = half.astype(bf16)
    rest = lax.ppermute(half, "acct", SECOND)
    own_scores, spread = call(
        far_kernel,
        [
            jax.ShapeDtypeStruct((SIDE, SIDE), bf16),
            jax.ShapeDtypeStruct((4, FOUR, SIDE), bf16),
        ],
        smem(1) + vmem(2),
        [],
        SIDE * SIDE * LINE,
        MEBI // 2,
    )(me, half, rest)

    g0 = lax.all_to_all(spread, "acct", 0, 0, tiled=True, axis_index_groups=QUADS)
    g0 = g0.reshape(LINE * SIDE, SIDE)
    g3 = lax.ppermute(g0, "acct", DIAGONAL)
    g1 = lax.ppermute(g0, "acct", BESIDE)
    g2 = lax.ppermute(g0, "acct", ACROSS)
    acc = jax.ShapeDtypeStruct((2 * ROWS, SIDE), f32)
    (before,) = call(
        functools.partial(backward_kernel, (0,), (0, 1)),
        [acc],
        smem(2) + vmem(3),
        [],
        flops,
        4 * MEBI,
    )(*slots, g0)

    def backward(half, dtype):
        (out,) = call(
            functools.partial(backward_kernel, (3, 1, 2), (half,)),
            [jax.ShapeDtypeStruct((ROWS, SIDE), dtype)],
            smem(1) + vmem(5),
            [pltpu.VMEM((ROWS, SIDE), f32)],
            flops,
            2 * MEBI,
        )(slots[half], slots[2 + half], g3, g1, g2, before)
        return out

    other = lax.ppermute(backward(1, bf16), "acct", SWAP)
    returned = (backward(0, f32) + other.astype(f32)).astype(bf16)
    types = jnp.broadcast_to(returned[None], (4, ROWS, SIDE))
    types = lax.all_to_all(types, "attr", 0, 0, tiled=True)
    (new_scores,) = call(
        finish_kernel,
        [jax.ShapeDtypeStruct((ROWS, SIDE), f32)],
        vmem(4),
        [],
        ROWS * SIDE * 8,
        MEBI,
    )(types, scores0, degree, seed_mask.reshape(4, SIDE))
    return (new_scores, own_scores[None])


def solution(mesh):
    placed = (
        P("acct", None),
        P("acct"),
        P("acct"),
        P("attr", "acct"),
        P("attr", "acct", None, None),
        P("attr", "acct"),
        P("attr", "acct"),
        P("attr", None),
        P("attr", "acct"),
    )
    return jax.shard_map(
        per_device,
        mesh=mesh,
        in_specs=placed,
        out_specs=(P("acct", None), P("attr", "acct", None)),
        check_vma=False,
    )
```

```python
import functools
import jax
import jax.numpy as jnp
from jax import lax
from jax.experimental import pallas as pl
from jax.experimental.pallas import tpu as pltpu
from jax.sharding import PartitionSpec as P

ALPHA = 0.8
SIDE = 128
SLOTS = 16
ROWS = 512
LINE = 16
MEBI = 2**20
TILES = SLOTS * SIDE
SENT = TILES + ROWS + SLOTS
FOUR = 4 * SIDE


def device(core, u, v):
    return (((u + core) % 16) * 4 + (v + core) % 4) * 2 + core


def pairs(meet):
    return [
        (device(c, u, v), device(c, *meet(c, u, v)))
        for c in range(2)
        for u in range(16)
        for v in range(4)
    ]


SWAP = [(i, i ^ 1) for i in range(128)]
BESIDE = pairs(lambda c, u, v: (u ^ 1, v))
ACROSS = pairs(lambda c, u, v: (u, v ^ 1))
DIAGONAL = pairs(lambda c, u, v: (u ^ 1, v ^ 1))
FIRST = pairs(lambda c, u, v: (u ^ 4 if c == 0 else 12 - (u & 12) + (u & 3), v))
SECOND = pairs(lambda c, u, v: (u ^ 4 if c == 1 else 12 - (u & 12) + (u & 3), v))
QUADS = [
    [device(c, far * 4 + step * 2 + odd, (0, 3, 1, 2)[side * 2 + end]) for end in (0, 1) for step in (0, 1)]
    for c in (0, 1)
    for side in (0, 1)
    for odd in (0, 1)
    for far in range(4)
]
def where(index):
    core = index & 1
    return core, ((index >> 3) - core) & 15, ((index >> 1) - core) & 3


def decode(owner, core, u, v):
    core1, u1, v1 = where(owner)
    side = (v ^ (v >> 1) ^ v1 ^ (v1 >> 1)) & 1
    chip = jnp.where(core1 == core, side * 2 + ((u ^ u1) & 1), 7)
    return chip * 16 + (v1 >> 1) * 8 + ((u1 >> 1) & 1) * 4 + (u1 >> 2)


def column(row):
    return jnp.broadcast_to(row, (SIDE, SIDE)).T


def prepare_kernel(me, table, attr, acct, count, weights, scores, degrees, payload, rows, degree, sems):
    tiles = pltpu.make_async_copy(weights, payload.at[pl.ds(0, TILES), :], sems.at[0])
    prior = pltpu.make_async_copy(scores, rows, sems.at[1])
    small = pltpu.make_async_copy(degrees, degree, sems.at[2])
    small.start()
    prior.start()
    tiles.start()
    core, u, v = where(me[0])
    twin, twin_u, twin_v = where(me[0] ^ 1)
    lane = lax.broadcasted_iota(jnp.int32, (SLOTS, SIDE), 1)
    tail = jnp.zeros((SLOTS, SIDE), jnp.int32)
    for s in range(SLOTS):
        owner = table[0, attr[0, s]]
        live = s < count[0, 0]
        tail = jnp.where(lane == s, jnp.where(live, decode(owner, core, u, v), 112), tail)
        sent = jnp.where(live, decode(owner, twin, twin_u, twin_v), 112)
        tail = jnp.where(lane == s + SLOTS, sent, tail)
        tail = jnp.where(lane == s + 2 * SLOTS, acct[0, s], tail)
    payload[TILES + ROWS :, :] = tail.astype(jnp.float32).astype(payload.dtype)
    small.wait()
    prior.wait()
    for n in range(4):
        scale = column(lax.rsqrt(degree[n : n + 1, :].astype(jnp.float32)))
        scaled = rows[pl.ds(n * SIDE, SIDE), :].astype(jnp.float32) * scale
        payload[pl.ds(TILES + n * SIDE, SIDE), :] = scaled.astype(payload.dtype)
    tiles.wait()


def tile(sent, s):
    return sent[pl.ds(pl.multiple_of(s * SIDE, SIDE), SIDE), :]


def forward_kernel(offsets, tail0, tail1, sent0, sent1, *refs):
    outs, acc = refs[:-1], refs[-1]
    acc[...] = jnp.zeros_like(acc)
    for half, (tail, sent) in enumerate(((tail0, sent0), (tail1, sent1))):

        def step(s, carry, half=half, tail=tail, sent=sent):
            code, block = tail[0, half * SLOTS + s], tail[0, 2 * SLOTS + s]
            chip, along = code >> 4, code & 15
            index = jnp.int32(0)
            wanted = jnp.bool_(False)
            for n, offset in enumerate(offsets):
                index = jnp.where(chip == offset, n * LINE, index)
                wanted = wanted | (chip == offset)

            @pl.when(wanted)
            def _():
                acc[index + along] += lax.dot_general(
                    tile(sent, s),
                    tile(sent, SLOTS + block),
                    (((0,), (0,)), ((), ())),
                    preferred_element_type=jnp.float32,
                )

            return carry

        lax.fori_loop(0, SLOTS, step, 0, unroll=True)
    for n, out in enumerate(outs):
        out[...] = acc[n * LINE : (n + 1) * LINE].astype(out.dtype)


def near_kernel(me, parts, degree, sums):
    for n in range(4):
        total = parts[0, n].astype(jnp.float32)
        for k in range(1, 4):
            total += parts[k, n].astype(jnp.float32)
        sums[n * SIDE : (n + 1) * SIDE, :] = total.astype(sums.dtype)
    row = lax.broadcasted_iota(jnp.int32, (SLOTS, SIDE), 0)
    mine = jnp.where(row == where(me[0])[1] >> 2, degree[...].astype(jnp.float32), 0.0)
    sums[FOUR:, :] = mine.astype(sums.dtype)


def far_kernel(me, mine, other, own, spread):
    degree = mine[FOUR:, :].astype(jnp.float32) + other[FOUR:, :].astype(jnp.float32)
    for n in range(4):
        rows = pl.ds(n * SIDE, SIDE)
        total = mine[rows, :].astype(jnp.float32) + other[rows, :].astype(jnp.float32)
        scores = (total * column(lax.rsqrt(degree[n : n + 1, :]))).astype(spread.dtype)
        for k in range(4):
            spread[k, rows, :] = scores
    far = where(me[0])[1] >> 2
    own[...] = spread[0, pl.ds(pl.multiple_of(far * SIDE, SIDE), SIDE), :]


def backward_kernel(chips, halves, *refs):
    tails, sents, refs = refs[: len(halves)], refs[len(halves) : 2 * len(halves)], refs[2 * len(halves) :]
    groups, refs = refs[: len(chips)], refs[len(chips) :]
    if len(refs) == 1:
        (acc,) = refs
        acc[...] = jnp.zeros_like(acc)
        base = 0
    else:
        before, out, acc = refs
        base = halves[0] * ROWS
        acc[...] = before[base : base + ROWS, :]
    for half, tail, sent in zip(halves, tails, sents):

        def step(s, carry, half=half, tail=tail, sent=sent):
            code, block = tail[0, half * SLOTS + s], tail[0, 2 * SLOTS + s]
            chip, along = code >> 4, code & 15
            for n, blocks in zip(chips, groups):

                @pl.when(chip == n)
                def _(blocks=blocks):
                    start = pl.multiple_of(half * ROWS - base + block * SIDE, SIDE)
                    acc[pl.ds(start, SIDE), :] += jnp.dot(
                        tile(sent, s), tile(blocks, along), preferred_element_type=jnp.float32
                    )

            return carry

        lax.fori_loop(0, SLOTS, step, 0, unroll=True)
    if len(refs) > 1:
        out[...] = acc[...].astype(out.dtype)


def finish_kernel(types, scores, degree, seed, new):
    for n in range(4):
        rows = pl.ds(n * SIDE, SIDE)
        scale = column(lax.rsqrt(degree[n : n + 1, :].astype(jnp.float32)))
        prior = scores[rows, :].astype(jnp.float32)
        whole = types[0, rows, :].astype(jnp.float32)
        for k in range(1, 4):
            whole += types[k, rows, :].astype(jnp.float32)
        mixed = ALPHA * (whole * scale) + (1.0 - ALPHA) * prior
        kept = column(seed[n : n + 1, :].astype(jnp.float32))
        new[rows, :] = jnp.where(kept == 1.0, prior, mixed)


def smem(n):
    return [pl.BlockSpec(memory_space=pltpu.SMEM)] * n


def vmem(n):
    return [pl.BlockSpec(memory_space=pltpu.VMEM)] * n


def call(kernel, outs, specs, scratch, flops, moved):
    return pl.pallas_call(
        kernel,
        out_shape=outs,
        in_specs=specs,
        out_specs=vmem(len(outs)),
        scratch_shapes=scratch,
        compiler_params=pltpu.CompilerParams(vmem_limit_bytes=24 * MEBI),
        cost_estimate=pl.CostEstimate(flops=flops, bytes_accessed=moved, transcendentals=0),
    )


def per_device(
    scores0,
    seed_mask,
    acct_degree,
    attr_degree,
    tile_weight,
    tile_acct,
    tile_attr,
    attr_owner,
    tile_count,
):
    bf16, f32, i32 = jnp.bfloat16, jnp.float32, jnp.int32
    group = jax.ShapeDtypeStruct((LINE, SIDE, SIDE), bf16)
    degree = acct_degree.reshape(4, SIDE)
    me = lax.axis_index("acct").astype(i32).reshape(1)
    (payload,) = call(
        prepare_kernel,
        [jax.ShapeDtypeStruct((SENT, SIDE), bf16)],
        smem(5) + [pl.BlockSpec(memory_space=pltpu.HBM)] * 3,
        [
            pltpu.VMEM((ROWS, SIDE), bf16),
            pltpu.VMEM((4, SIDE), i32),
            pltpu.SemaphoreType.DMA((3,)),
        ],
        ROWS * SIDE,
        MEBI,
    )(
        me,
        attr_owner,
        tile_attr,
        tile_acct,
        tile_count,
        *(
            pltpu.with_memory_space_constraint(array, pltpu.HBM)
            for array in (tile_weight.reshape(TILES, SIDE), scores0, degree)
        ),
    )
    payload1 = lax.ppermute(payload, "acct", SWAP)
    flops = 2 * 10 * SIDE**3
    tails = [sent[TILES + ROWS :][:1].astype(i32) for sent in (payload, payload1)]
    slots = (*tails, payload, payload1)

    def forward(chips):
        return call(
            functools.partial(forward_kernel, chips),
            [group] * len(chips),
            smem(2) + vmem(2),
            [pltpu.VMEM((len(chips) * LINE, SIDE, SIDE), f32)],
            flops,
            3 * MEBI,
        )(*slots)

    o3, o1, o2 = forward((3, 1, 2))
    r3 = lax.ppermute(o3, "acct", DIAGONAL)
    r1 = lax.ppermute(o1, "acct", BESIDE)
    r2 = lax.ppermute(o2, "acct", ACROSS)
    (o0,) = forward((0,))
    line = o0.astype(f32) + r1.astype(f32) + r2.astype(f32) + r3.astype(f32)
    line = line.astype(bf16).reshape(4, 4, SIDE, SIDE)
    line = lax.all_to_all(line, "acct", 0, 0, tiled=True, axis_index_groups=QUADS)
    sums = jax.ShapeDtypeStruct((FOUR + SLOTS, SIDE), bf16)
    (near,) = call(
        near_kernel, [sums], smem(1) + vmem(2), [], SIDE * SIDE * LINE, MEBI
    )(me, line, attr_degree)
    half = near.astype(f32) + lax.ppermute(near, "acct", FIRST).astype(f32)
    half = half.astype(bf16)
    rest = lax.ppermute(half, "acct", SECOND)
    own_scores, spread = call(
        far_kernel,
        [
            jax.ShapeDtypeStruct((SIDE, SIDE), bf16),
            jax.ShapeDtypeStruct((4, FOUR, SIDE), bf16),
        ],
        smem(1) + vmem(2),
        [],
        SIDE * SIDE * LINE,
        MEBI // 2,
    )(me, half, rest)

    g0 = lax.all_to_all(spread, "acct", 0, 0, tiled=True, axis_index_groups=QUADS)
    g0 = g0.reshape(LINE * SIDE, SIDE)
    g3 = lax.ppermute(g0, "acct", DIAGONAL)
    g2 = lax.ppermute(g0, "acct", ACROSS)
    g1 = lax.ppermute(g0, "acct", BESIDE)
    acc = jax.ShapeDtypeStruct((2 * ROWS, SIDE), f32)
    (before,) = call(
        functools.partial(backward_kernel, (0,), (0, 1)),
        [acc],
        smem(2) + vmem(3),
        [],
        flops,
        4 * MEBI,
    )(*slots, g0)

    def backward(half, dtype):
        (out,) = call(
            functools.partial(backward_kernel, (3, 2, 1), (half,)),
            [jax.ShapeDtypeStruct((ROWS, SIDE), dtype)],
            smem(1) + vmem(5),
            [pltpu.VMEM((ROWS, SIDE), f32)],
            flops,
            2 * MEBI,
        )(slots[half], slots[2 + half], g3, g2, g1, before)
        return out

    other = lax.ppermute(backward(1, bf16), "acct", SWAP)
    returned = (backward(0, f32) + other.astype(f32)).astype(bf16)
    types = jnp.broadcast_to(returned[None], (4, ROWS, SIDE))
    types = lax.all_to_all(types, "attr", 0, 0, tiled=True)
    (new_scores,) = call(
        finish_kernel,
        [jax.ShapeDtypeStruct((ROWS, SIDE), f32)],
        vmem(4),
        [],
        ROWS * SIDE * 8,
        MEBI,
    )(types, scores0, degree, seed_mask.reshape(4, SIDE))
    return (new_scores, own_scores[None])


def solution(mesh):
    placed = (
        P("acct", None),
        P("acct"),
        P("acct"),
        P("attr", "acct"),
        P("attr", "acct", None, None),
        P("attr", "acct"),
        P("attr", "acct"),
        P("attr", None),
        P("attr", "acct"),
    )
    return jax.shard_map(
        per_device,
        mesh=mesh,
        in_specs=placed,
        out_specs=(P("acct", None), P("attr", "acct", None)),
        check_vma=False,
    )
```

```python
import functools
import jax
import jax.numpy as jnp
from jax import lax
from jax.experimental import pallas as pl
from jax.experimental.pallas import tpu as pltpu
from jax.sharding import PartitionSpec as P

ALPHA = 0.8
SIDE = 128
SLOTS = 16
ROWS = 512
LINE = 16
MEBI = 2**20
TILES = SLOTS * SIDE
SENT = TILES + ROWS + SLOTS
FOUR = 4 * SIDE


def device(core, u, v):
    return (((u + core) % 16) * 4 + (v + core) % 4) * 2 + core


def pairs(meet):
    return [
        (device(c, u, v), device(c, *meet(c, u, v)))
        for c in range(2)
        for u in range(16)
        for v in range(4)
    ]


SWAP = [(i, i ^ 1) for i in range(128)]
BESIDE = pairs(lambda c, u, v: (u ^ 1, v))
ACROSS = pairs(lambda c, u, v: (u, v ^ 1))
DIAGONAL = pairs(lambda c, u, v: (u ^ 1, v ^ 1))
FIRST = pairs(lambda c, u, v: (u ^ 4 if c == 0 else 12 - (u & 12) + (u & 3), v))
SECOND = pairs(lambda c, u, v: (u ^ 4 if c == 1 else 12 - (u & 12) + (u & 3), v))
QUADS = [
    [device(c, far * 4 + step * 2 + odd, (0, 3, 1, 2)[side * 2 + end]) for end in (0, 1) for step in (0, 1)]
    for c in (0, 1)
    for side in (0, 1)
    for odd in (0, 1)
    for far in range(4)
]
def where(index):
    core = index & 1
    return core, ((index >> 3) - core) & 15, ((index >> 1) - core) & 3


def decode(owner, core, u, v):
    core1, u1, v1 = where(owner)
    side = (v ^ (v >> 1) ^ v1 ^ (v1 >> 1)) & 1
    chip = jnp.where(core1 == core, side * 2 + ((u ^ u1) & 1), 7)
    return chip * 16 + (v1 >> 1) * 8 + ((u1 >> 1) & 1) * 4 + (u1 >> 2)


def column(row):
    return jnp.broadcast_to(row, (SIDE, SIDE)).T


def prepare_kernel(me, count, *refs):
    tables, (weights, scores, degrees, payload) = refs[:3], refs[3:7]
    table, attr, acct, rows, degree, sems = refs[7:]
    small = [
        pltpu.make_async_copy(source, target, sems.at[n])
        for n, (source, target) in enumerate(zip((*tables, degrees), (table, attr, acct, degree)))
    ]
    for copy in small:
        copy.start()
    tiles = pltpu.make_async_copy(weights, payload.at[pl.ds(0, TILES), :], sems.at[4])
    prior = pltpu.make_async_copy(scores, rows, sems.at[5])
    prior.start()
    tiles.start()
    for copy in small:
        copy.wait()
    core, u, v = where(me[0])
    twin, twin_u, twin_v = where(me[0] ^ 1)
    lane = lax.broadcasted_iota(jnp.int32, (SLOTS, SIDE), 1)
    tail = jnp.zeros((SLOTS, SIDE), jnp.int32)
    for s in range(SLOTS):
        owner = table[0, attr[0, s]]
        live = s < count[0, 0]
        tail = jnp.where(lane == s, jnp.where(live, decode(owner, core, u, v), 112), tail)
        sent = jnp.where(live, decode(owner, twin, twin_u, twin_v), 112)
        tail = jnp.where(lane == s + SLOTS, sent, tail)
        tail = jnp.where(lane == s + 2 * SLOTS, acct[0, s], tail)
    payload[TILES + ROWS :, :] = tail.astype(jnp.float32).astype(payload.dtype)
    prior.wait()
    for n in range(4):
        scale = column(lax.rsqrt(degree[n : n + 1, :].astype(jnp.float32)))
        scaled = rows[pl.ds(n * SIDE, SIDE), :].astype(jnp.float32) * scale
        payload[pl.ds(TILES + n * SIDE, SIDE), :] = scaled.astype(payload.dtype)
    tiles.wait()


def tile(sent, s):
    return sent[pl.ds(pl.multiple_of(s * SIDE, SIDE), SIDE), :]


def forward_kernel(offsets, tail0, tail1, sent0, sent1, *refs):
    outs, acc = refs[:-1], refs[-1]
    acc[...] = jnp.zeros_like(acc)
    for half, (tail, sent) in enumerate(((tail0, sent0), (tail1, sent1))):

        def step(s, carry, half=half, tail=tail, sent=sent):
            code, block = tail[0, half * SLOTS + s], tail[0, 2 * SLOTS + s]
            chip, along = code >> 4, code & 15
            index = jnp.int32(0)
            wanted = jnp.bool_(False)
            for n, offset in enumerate(offsets):
                index = jnp.where(chip == offset, n * LINE, index)
                wanted = wanted | (chip == offset)

            @pl.when(wanted)
            def _():
                acc[index + along] += lax.dot_general(
                    tile(sent, s),
                    tile(sent, SLOTS + block),
                    (((0,), (0,)), ((), ())),
                    preferred_element_type=jnp.float32,
                )

            return carry

        lax.fori_loop(0, SLOTS, step, 0, unroll=True)
    for n, out in enumerate(outs):
        out[...] = acc[n * LINE : (n + 1) * LINE].astype(out.dtype)


def near_kernel(me, parts, degree, sums, sent):
    for n in range(4):
        total = parts[0, n].astype(jnp.float32)
        for k in range(1, 4):
            total += parts[k, n].astype(jnp.float32)
        sums[n * SIDE : (n + 1) * SIDE, :] = total
        sent[n * SIDE : (n + 1) * SIDE, :] = total.astype(sent.dtype)
    row = lax.broadcasted_iota(jnp.int32, (SLOTS, SIDE), 0)
    mine = jnp.where(row == where(me[0])[1] >> 2, degree[...].astype(jnp.float32), 0.0)
    sums[FOUR:, :] = mine
    sent[FOUR:, :] = mine.astype(sent.dtype)


def far_kernel(me, mine, other, own, spread):
    degree = mine[FOUR:, :] + other[FOUR:, :].astype(jnp.float32)
    for n in range(4):
        rows = pl.ds(n * SIDE, SIDE)
        total = mine[rows, :] + other[rows, :].astype(jnp.float32)
        scores = (total * column(lax.rsqrt(degree[n : n + 1, :]))).astype(spread.dtype)
        for k in range(4):
            spread[k, rows, :] = scores
    far = where(me[0])[1] >> 2
    own[...] = spread[0, pl.ds(pl.multiple_of(far * SIDE, SIDE), SIDE), :]


def backward_kernel(chips, halves, *refs):
    tails, sents, refs = refs[: len(halves)], refs[len(halves) : 2 * len(halves)], refs[2 * len(halves) :]
    groups, refs = refs[: len(chips)], refs[len(chips) :]
    if len(refs) == 1:
        (acc,) = refs
        acc[...] = jnp.zeros_like(acc)
        base = 0
    else:
        before, out, acc = refs
        base = halves[0] * ROWS
        acc[...] = before[base : base + ROWS, :]
    for half, tail, sent in zip(halves, tails, sents):

        def step(s, carry, half=half, tail=tail, sent=sent):
            code, block = tail[0, half * SLOTS + s], tail[0, 2 * SLOTS + s]
            chip, along = code >> 4, code & 15
            for n, blocks in zip(chips, groups):

                @pl.when(chip == n)
                def _(blocks=blocks):
                    start = pl.multiple_of(half * ROWS - base + block * SIDE, SIDE)
                    acc[pl.ds(start, SIDE), :] += jnp.dot(
                        tile(sent, s), tile(blocks, along), preferred_element_type=jnp.float32
                    )

            return carry

        lax.fori_loop(0, SLOTS, step, 0, unroll=True)
    if len(refs) > 1:
        out[...] = acc[...].astype(out.dtype)


def finish_kernel(types, scores, degree, seed, new):
    for n in range(4):
        rows = pl.ds(n * SIDE, SIDE)
        scale = column(lax.rsqrt(degree[n : n + 1, :].astype(jnp.float32)))
        prior = scores[rows, :].astype(jnp.float32)
        whole = types[0, rows, :].astype(jnp.float32)
        for k in range(1, 4):
            whole += types[k, rows, :].astype(jnp.float32)
        mixed = ALPHA * (whole * scale) + (1.0 - ALPHA) * prior
        kept = column(seed[n : n + 1, :].astype(jnp.float32))
        new[rows, :] = jnp.where(kept == 1.0, prior, mixed)


def smem(n):
    return [pl.BlockSpec(memory_space=pltpu.SMEM)] * n


def vmem(n):
    return [pl.BlockSpec(memory_space=pltpu.VMEM)] * n


def call(kernel, outs, specs, scratch, flops, moved):
    return pl.pallas_call(
        kernel,
        out_shape=outs,
        in_specs=specs,
        out_specs=vmem(len(outs)),
        scratch_shapes=scratch,
        compiler_params=pltpu.CompilerParams(vmem_limit_bytes=24 * MEBI),
        cost_estimate=pl.CostEstimate(flops=flops, bytes_accessed=moved, transcendentals=0),
    )


def per_device(
    scores0,
    seed_mask,
    acct_degree,
    attr_degree,
    tile_weight,
    tile_acct,
    tile_attr,
    attr_owner,
    tile_count,
):
    bf16, f32, i32 = jnp.bfloat16, jnp.float32, jnp.int32
    degree = acct_degree.reshape(4, SIDE)
    me = lax.axis_index("acct").astype(i32).reshape(1)
    (payload,) = call(
        prepare_kernel,
        [jax.ShapeDtypeStruct((SENT, SIDE), bf16)],
        smem(2) + [pl.BlockSpec(memory_space=pltpu.HBM)] * 6,
        [
            pltpu.SMEM((1, SIDE), i32),
            pltpu.SMEM((1, SLOTS), i32),
            pltpu.SMEM((1, SLOTS), i32),
            pltpu.VMEM((ROWS, SIDE), bf16),
            pltpu.VMEM((4, SIDE), i32),
            pltpu.SemaphoreType.DMA((6,)),
        ],
        ROWS * SIDE,
        MEBI,
    )(
        me,
        tile_count,
        *(
            pltpu.with_memory_space_constraint(array, pltpu.HBM)
            for array in (
                attr_owner,
                tile_attr,
                tile_acct,
                tile_weight.reshape(TILES, SIDE),
                scores0,
                degree,
            )
        ),
    )
    payload1 = lax.ppermute(payload, "acct", SWAP)
    flops = 2 * 10 * SIDE**3
    tails = [sent[TILES + ROWS :][:1].astype(i32) for sent in (payload, payload1)]
    slots = (*tails, payload, payload1)

    def forward(chips, dtype):
        return call(
            functools.partial(forward_kernel, chips),
            [jax.ShapeDtypeStruct((LINE, SIDE, SIDE), dtype)] * len(chips),
            smem(2) + vmem(2),
            [pltpu.VMEM((len(chips) * LINE, SIDE, SIDE), f32)],
            flops,
            3 * MEBI,
        )(*slots)

    o3, o1, o2 = forward((3, 1, 2), bf16)
    r3 = lax.ppermute(o3, "acct", DIAGONAL)
    r1 = lax.ppermute(o1, "acct", BESIDE)
    r2 = lax.ppermute(o2, "acct", ACROSS)
    (o0,) = forward((0,), f32)
    line = o0 + r3.astype(f32) + r2.astype(f32) + r1.astype(f32)
    line = line.astype(bf16).reshape(4, 4, SIDE, SIDE)
    line = lax.all_to_all(line, "acct", 0, 0, tiled=True, axis_index_groups=QUADS)
    near, sent = call(
        near_kernel,
        [jax.ShapeDtypeStruct((FOUR + SLOTS, SIDE), dtype) for dtype in (f32, bf16)],
        smem(1) + vmem(2),
        [],
        SIDE * SIDE * LINE,
        MEBI,
    )(me, line, attr_degree)
    half = near + lax.ppermute(sent, "acct", FIRST).astype(f32)
    rest = lax.ppermute(half.astype(bf16), "acct", SECOND)
    own_scores, spread = call(
        far_kernel,
        [
            jax.ShapeDtypeStruct((SIDE, SIDE), bf16),
            jax.ShapeDtypeStruct((4, FOUR, SIDE), bf16),
        ],
        smem(1) + vmem(2),
        [],
        SIDE * SIDE * LINE,
        MEBI // 2,
    )(me, half, rest)

    g0 = lax.all_to_all(spread, "acct", 0, 0, tiled=True, axis_index_groups=QUADS)
    g0 = g0.reshape(LINE * SIDE, SIDE)
    g3 = lax.ppermute(g0, "acct", DIAGONAL)
    g1 = lax.ppermute(g0, "acct", BESIDE)
    g2 = lax.ppermute(g0, "acct", ACROSS)
    acc = jax.ShapeDtypeStruct((2 * ROWS, SIDE), f32)
    (before,) = call(
        functools.partial(backward_kernel, (0,), (0, 1)),
        [acc],
        smem(2) + vmem(3),
        [],
        flops,
        4 * MEBI,
    )(*slots, g0)

    def backward(half, dtype):
        (out,) = call(
            functools.partial(backward_kernel, (3, 1, 2), (half,)),
            [jax.ShapeDtypeStruct((ROWS, SIDE), dtype)],
            smem(1) + vmem(5),
            [pltpu.VMEM((ROWS, SIDE), f32)],
            flops,
            2 * MEBI,
        )(slots[half], slots[2 + half], g3, g1, g2, before)
        return out

    other = lax.ppermute(backward(1, bf16), "acct", SWAP)
    returned = (backward(0, f32) + other.astype(f32)).astype(bf16)
    types = jnp.broadcast_to(returned[None], (4, ROWS, SIDE))
    types = lax.all_to_all(types, "attr", 0, 0, tiled=True)
    (new_scores,) = call(
        finish_kernel,
        [jax.ShapeDtypeStruct((ROWS, SIDE), f32)],
        vmem(4),
        [],
        ROWS * SIDE * 8,
        MEBI,
    )(types, scores0, degree, seed_mask.reshape(4, SIDE))
    return (new_scores, own_scores[None])


def solution(mesh):
    placed = (
        P("acct", None),
        P("acct"),
        P("acct"),
        P("attr", "acct"),
        P("attr", "acct", None, None),
        P("attr", "acct"),
        P("attr", "acct"),
        P("attr", None),
        P("attr", "acct"),
    )
    return jax.shard_map(
        per_device,
        mesh=mesh,
        in_specs=placed,
        out_specs=(P("acct", None), P("attr", "acct", None)),
        check_vma=False,
    )
```

```python
import functools
import jax
import jax.numpy as jnp
from jax import lax
from jax.experimental import pallas as pl
from jax.experimental.pallas import tpu as pltpu
from jax.sharding import PartitionSpec as P

ALPHA = 0.8
SIDE = 128
SLOTS = 16
ROWS = 512
LINE = 16
MEBI = 2**20
TILES = SLOTS * SIDE
SENT = TILES + ROWS + SLOTS
FOUR = 4 * SIDE


def device(core, u, v):
    return (((u + core) % 16) * 4 + (v + core) % 4) * 2 + core


def pairs(meet):
    return [
        (device(c, u, v), device(c, *meet(c, u, v)))
        for c in range(2)
        for u in range(16)
        for v in range(4)
    ]


SWAP = [(i, i ^ 1) for i in range(128)]
BESIDE = pairs(lambda c, u, v: (u ^ 1, v))
ACROSS = pairs(lambda c, u, v: (u, v ^ 1))
DIAGONAL = pairs(lambda c, u, v: (u ^ 1, v ^ 1))
FIRST = pairs(lambda c, u, v: (u ^ 4 if c == 0 else 12 - (u & 12) + (u & 3), v))
SECOND = pairs(lambda c, u, v: (u ^ 4 if c == 1 else 12 - (u & 12) + (u & 3), v))
QUADS = [
    [device(c, far * 4 + step * 2 + odd, (0, 3, 1, 2)[side * 2 + end]) for end in (0, 1) for step in (0, 1)]
    for c in (0, 1)
    for side in (0, 1)
    for odd in (0, 1)
    for far in range(4)
]
def where(index):
    core = index & 1
    return core, ((index >> 3) - core) & 15, ((index >> 1) - core) & 3


def decode(owner, core, u, v):
    core1, u1, v1 = where(owner)
    side = (v ^ (v >> 1) ^ v1 ^ (v1 >> 1)) & 1
    chip = jnp.where(core1 == core, side * 2 + ((u ^ u1) & 1), 7)
    return chip * 16 + (v1 >> 1) * 8 + ((u1 >> 1) & 1) * 4 + (u1 >> 2)


def column(row):
    return jnp.broadcast_to(row, (SIDE, SIDE)).T


def prepare_kernel(me, count, *refs):
    tables, (weights, scores, degrees, payload) = refs[:3], refs[3:7]
    table, attr, acct, rows, degree, sems = refs[7:]
    small = [
        pltpu.make_async_copy(source, target, sems.at[n])
        for n, (source, target) in enumerate(zip((*tables, degrees), (table, attr, acct, degree)))
    ]
    for copy in small:
        copy.start()
    tiles = pltpu.make_async_copy(weights, payload.at[pl.ds(0, TILES), :], sems.at[4])
    prior = pltpu.make_async_copy(scores, rows, sems.at[5])
    prior.start()
    tiles.start()
    for copy in small:
        copy.wait()
    core, u, v = where(me[0])
    twin, twin_u, twin_v = where(me[0] ^ 1)
    lane = lax.broadcasted_iota(jnp.int32, (SLOTS, SIDE), 1)
    tail = jnp.zeros((SLOTS, SIDE), jnp.int32)
    for s in range(SLOTS):
        owner = table[0, attr[0, s]]
        live = s < count[0, 0]
        tail = jnp.where(lane == s, jnp.where(live, decode(owner, core, u, v), 112), tail)
        sent = jnp.where(live, decode(owner, twin, twin_u, twin_v), 112)
        tail = jnp.where(lane == s + SLOTS, sent, tail)
        tail = jnp.where(lane == s + 2 * SLOTS, acct[0, s], tail)
    payload[TILES + ROWS :, :] = tail.astype(jnp.float32).astype(payload.dtype)
    prior.wait()
    for n in range(4):
        scale = column(lax.rsqrt(degree[n : n + 1, :].astype(jnp.float32)))
        scaled = rows[pl.ds(n * SIDE, SIDE), :].astype(jnp.float32) * scale
        payload[pl.ds(TILES + n * SIDE, SIDE), :] = scaled.astype(payload.dtype)
    tiles.wait()


def tile(sent, s):
    return sent[pl.ds(pl.multiple_of(s * SIDE, SIDE), SIDE), :]


def forward_kernel(offsets, tail0, tail1, sent0, sent1, *refs):
    outs, acc = refs[:-1], refs[-1]
    acc[...] = jnp.zeros_like(acc)
    for half, (tail, sent) in enumerate(((tail0, sent0), (tail1, sent1))):

        def step(s, carry, half=half, tail=tail, sent=sent):
            code, block = tail[0, half * SLOTS + s], tail[0, 2 * SLOTS + s]
            chip, along = code >> 4, code & 15
            index = jnp.int32(0)
            wanted = jnp.bool_(False)
            for n, offset in enumerate(offsets):
                index = jnp.where(chip == offset, n * LINE, index)
                wanted = wanted | (chip == offset)

            @pl.when(wanted)
            def _():
                acc[index + along] += lax.dot_general(
                    tile(sent, s),
                    tile(sent, SLOTS + block),
                    (((0,), (0,)), ((), ())),
                    preferred_element_type=jnp.float32,
                )

            return carry

        lax.fori_loop(0, SLOTS, step, 0, unroll=True)
    for n, out in enumerate(outs):
        out[...] = acc[n * LINE : (n + 1) * LINE].astype(out.dtype)


def near_kernel(me, parts, degree, sums, sent):
    for n in range(4):
        total = parts[0, n].astype(jnp.float32)
        for k in range(1, 4):
            total += parts[k, n].astype(jnp.float32)
        sums[n * SIDE : (n + 1) * SIDE, :] = total
        sent[n * SIDE : (n + 1) * SIDE, :] = total.astype(sent.dtype)
    row = lax.broadcasted_iota(jnp.int32, (SLOTS, SIDE), 0)
    mine = jnp.where(row == where(me[0])[1] >> 2, degree[...].astype(jnp.float32), 0.0)
    sums[FOUR:, :] = mine
    sent[FOUR:, :] = mine.astype(sent.dtype)


def far_kernel(me, mine, other, own, spread):
    degree = mine[FOUR:, :] + other[FOUR:, :].astype(jnp.float32)
    for n in range(4):
        rows = pl.ds(n * SIDE, SIDE)
        total = mine[rows, :] + other[rows, :].astype(jnp.float32)
        scores = (total * column(lax.rsqrt(degree[n : n + 1, :]))).astype(spread.dtype)
        for k in range(4):
            spread[k, rows, :] = scores
    far = where(me[0])[1] >> 2
    own[...] = spread[0, pl.ds(pl.multiple_of(far * SIDE, SIDE), SIDE), :]


def backward_kernel(chips, halves, *refs):
    tails, sents, refs = refs[: len(halves)], refs[len(halves) : 2 * len(halves)], refs[2 * len(halves) :]
    groups, refs = refs[: len(chips)], refs[len(chips) :]
    if len(refs) == 1:
        (acc,) = refs
        acc[...] = jnp.zeros_like(acc)
        base = 0
    else:
        before, out, acc = refs
        base = halves[0] * ROWS
        acc[...] = before[base : base + ROWS, :]
    for half, tail, sent in zip(halves, tails, sents):

        def step(s, carry, half=half, tail=tail, sent=sent):
            code, block = tail[0, half * SLOTS + s], tail[0, 2 * SLOTS + s]
            chip, along = code >> 4, code & 15
            for n, blocks in zip(chips, groups):

                @pl.when(chip == n)
                def _(blocks=blocks):
                    start = pl.multiple_of(half * ROWS - base + block * SIDE, SIDE)
                    acc[pl.ds(start, SIDE), :] += jnp.dot(
                        tile(sent, s), tile(blocks, along), preferred_element_type=jnp.float32
                    )

            return carry

        lax.fori_loop(0, SLOTS, step, 0, unroll=True)
    if len(refs) > 1:
        out[...] = acc[...].astype(out.dtype)


def finish_kernel(types, scores, degree, seed, new):
    for n in range(4):
        rows = pl.ds(n * SIDE, SIDE)
        scale = column(lax.rsqrt(degree[n : n + 1, :].astype(jnp.float32)))
        prior = scores[rows, :].astype(jnp.float32)
        whole = types[0, rows, :].astype(jnp.float32)
        for k in range(1, 4):
            whole += types[k, rows, :].astype(jnp.float32)
        mixed = ALPHA * (whole * scale) + (1.0 - ALPHA) * prior
        kept = column(seed[n : n + 1, :].astype(jnp.float32))
        new[rows, :] = jnp.where(kept == 1.0, prior, mixed)


def smem(n):
    return [pl.BlockSpec(memory_space=pltpu.SMEM)] * n


def vmem(n):
    return [pl.BlockSpec(memory_space=pltpu.VMEM)] * n


def call(kernel, outs, specs, scratch, flops, moved):
    return pl.pallas_call(
        kernel,
        out_shape=outs,
        in_specs=specs,
        out_specs=vmem(len(outs)),
        scratch_shapes=scratch,
        compiler_params=pltpu.CompilerParams(vmem_limit_bytes=24 * MEBI),
        cost_estimate=pl.CostEstimate(flops=flops, bytes_accessed=moved, transcendentals=0),
    )


def per_device(
    scores0,
    seed_mask,
    acct_degree,
    attr_degree,
    tile_weight,
    tile_acct,
    tile_attr,
    attr_owner,
    tile_count,
):
    bf16, f32, i32 = jnp.bfloat16, jnp.float32, jnp.int32
    degree = acct_degree.reshape(4, SIDE)
    me = lax.axis_index("acct").astype(i32).reshape(1)
    (payload,) = call(
        prepare_kernel,
        [jax.ShapeDtypeStruct((SENT, SIDE), bf16)],
        smem(2) + [pl.BlockSpec(memory_space=pltpu.HBM)] * 6,
        [
            pltpu.SMEM((1, SIDE), i32),
            pltpu.SMEM((1, SLOTS), i32),
            pltpu.SMEM((1, SLOTS), i32),
            pltpu.VMEM((ROWS, SIDE), bf16),
            pltpu.VMEM((4, SIDE), i32),
            pltpu.SemaphoreType.DMA((6,)),
        ],
        ROWS * SIDE,
        MEBI,
    )(
        me,
        tile_count,
        *(
            pltpu.with_memory_space_constraint(array, pltpu.HBM)
            for array in (
                attr_owner,
                tile_attr,
                tile_acct,
                tile_weight.reshape(TILES, SIDE),
                scores0,
                degree,
            )
        ),
    )
    payload1 = lax.ppermute(payload, "acct", SWAP)
    flops = 2 * 10 * SIDE**3
    tails = [sent[TILES + ROWS :][:1].astype(i32) for sent in (payload, payload1)]
    slots = (*tails, payload, payload1)

    def forward(chips, dtype):
        return call(
            functools.partial(forward_kernel, chips),
            [jax.ShapeDtypeStruct((LINE, SIDE, SIDE), dtype)] * len(chips),
            smem(2) + vmem(2),
            [pltpu.VMEM((len(chips) * LINE, SIDE, SIDE), f32)],
            flops,
            3 * MEBI,
        )(*slots)

    (o3,) = forward((3,), bf16)
    r3 = lax.ppermute(o3, "acct", DIAGONAL)
    (o2,) = forward((2,), bf16)
    r2 = lax.ppermute(o2, "acct", ACROSS)
    (o1,) = forward((1,), bf16)
    r1 = lax.ppermute(o1, "acct", BESIDE)
    (o0,) = forward((0,), f32)
    line = o0 + r3.astype(f32) + r2.astype(f32) + r1.astype(f32)
    line = line.astype(bf16).reshape(4, 4, SIDE, SIDE)
    line = lax.all_to_all(line, "acct", 0, 0, tiled=True, axis_index_groups=QUADS)
    near, sent = call(
        near_kernel,
        [jax.ShapeDtypeStruct((FOUR + SLOTS, SIDE), dtype) for dtype in (f32, bf16)],
        smem(1) + vmem(2),
        [],
        SIDE * SIDE * LINE,
        MEBI,
    )(me, line, attr_degree)
    half = near + lax.ppermute(sent, "acct", FIRST).astype(f32)
    rest = lax.ppermute(half.astype(bf16), "acct", SECOND)
    own_scores, spread = call(
        far_kernel,
        [
            jax.ShapeDtypeStruct((SIDE, SIDE), bf16),
            jax.ShapeDtypeStruct((4, FOUR, SIDE), bf16),
        ],
        smem(1) + vmem(2),
        [],
        SIDE * SIDE * LINE,
        MEBI // 2,
    )(me, half, rest)

    g0 = lax.all_to_all(spread, "acct", 0, 0, tiled=True, axis_index_groups=QUADS)
    g0 = g0.reshape(LINE * SIDE, SIDE)
    g3 = lax.ppermute(g0, "acct", DIAGONAL)
    g1 = lax.ppermute(g0, "acct", BESIDE)
    g2 = lax.ppermute(g0, "acct", ACROSS)
    acc = jax.ShapeDtypeStruct((2 * ROWS, SIDE), f32)
    (before,) = call(
        functools.partial(backward_kernel, (0,), (0, 1)),
        [acc],
        smem(2) + vmem(3),
        [],
        flops,
        4 * MEBI,
    )(*slots, g0)

    def backward(half, dtype):
        (out,) = call(
            functools.partial(backward_kernel, (3, 1, 2), (half,)),
            [jax.ShapeDtypeStruct((ROWS, SIDE), dtype)],
            smem(1) + vmem(5),
            [pltpu.VMEM((ROWS, SIDE), f32)],
            flops,
            2 * MEBI,
        )(slots[half], slots[2 + half], g3, g1, g2, before)
        return out

    other = lax.ppermute(backward(1, bf16), "acct", SWAP)
    returned = (backward(0, f32) + other.astype(f32)).astype(bf16)
    types = jnp.broadcast_to(returned[None], (4, ROWS, SIDE))
    types = lax.all_to_all(types, "attr", 0, 0, tiled=True)
    (new_scores,) = call(
        finish_kernel,
        [jax.ShapeDtypeStruct((ROWS, SIDE), f32)],
        vmem(4),
        [],
        ROWS * SIDE * 8,
        MEBI,
    )(types, scores0, degree, seed_mask.reshape(4, SIDE))
    return (new_scores, own_scores[None])


def solution(mesh):
    placed = (
        P("acct", None),
        P("acct"),
        P("acct"),
        P("attr", "acct"),
        P("attr", "acct", None, None),
        P("attr", "acct"),
        P("attr", "acct"),
        P("attr", None),
        P("attr", "acct"),
    )
    return jax.shard_map(
        per_device,
        mesh=mesh,
        in_specs=placed,
        out_specs=(P("acct", None), P("attr", "acct", None)),
        check_vma=False,
    )
```

```python
import functools
import jax
import jax.numpy as jnp
from jax import lax
from jax.experimental import pallas as pl
from jax.experimental.pallas import tpu as pltpu
from jax.sharding import PartitionSpec as P

ALPHA = 0.8
SIDE = 128
SLOTS = 16
ROWS = 512
LINE = 16
MEBI = 2**20
TILES = SLOTS * SIDE
SENT = TILES + ROWS + SLOTS
FOUR = 4 * SIDE


def device(core, u, v):
    return (((u + core) % 16) * 4 + (v + core) % 4) * 2 + core


def pairs(meet):
    return [
        (device(c, u, v), device(c, *meet(c, u, v)))
        for c in range(2)
        for u in range(16)
        for v in range(4)
    ]


SWAP = [(i, i ^ 1) for i in range(128)]
BESIDE = pairs(lambda c, u, v: (u ^ 1, v))
ACROSS = pairs(lambda c, u, v: (u, v ^ 1))
DIAGONAL = pairs(lambda c, u, v: (u ^ 1, v ^ 1))
FIRST = pairs(lambda c, u, v: (u ^ 4 if c == 0 else 12 - (u & 12) + (u & 3), v))
SECOND = pairs(lambda c, u, v: (u ^ 4 if c == 1 else 12 - (u & 12) + (u & 3), v))
QUADS = [
    [device(c, far * 4 + step * 2 + odd, (0, 3, 1, 2)[side * 2 + end]) for end in (0, 1) for step in (0, 1)]
    for c in (0, 1)
    for side in (0, 1)
    for odd in (0, 1)
    for far in range(4)
]
def where(index):
    core = index & 1
    return core, ((index >> 3) - core) & 15, ((index >> 1) - core) & 3


def decode(owner, core, u, v):
    core1, u1, v1 = where(owner)
    side = (v ^ (v >> 1) ^ v1 ^ (v1 >> 1)) & 1
    chip = jnp.where(core1 == core, side * 2 + ((u ^ u1) & 1), 7)
    return chip * 16 + (v1 >> 1) * 8 + ((u1 >> 1) & 1) * 4 + (u1 >> 2)


def column(row):
    return jnp.broadcast_to(row, (SIDE, SIDE)).T


def prepare_kernel(me, count, *refs):
    tables, (weights, scores, degrees, payload) = refs[:3], refs[3:7]
    table, attr, acct, rows, degree, sems = refs[7:]
    small = [
        pltpu.make_async_copy(source, target, sems.at[n])
        for n, (source, target) in enumerate(zip((*tables, degrees), (table, attr, acct, degree)))
    ]
    for copy in small:
        copy.start()
    tiles = pltpu.make_async_copy(weights, payload.at[pl.ds(0, TILES), :], sems.at[4])
    prior = pltpu.make_async_copy(scores, rows, sems.at[5])
    prior.start()
    tiles.start()
    for copy in small:
        copy.wait()
    core, u, v = where(me[0])
    twin, twin_u, twin_v = where(me[0] ^ 1)
    lane = lax.broadcasted_iota(jnp.int32, (SLOTS, SIDE), 1)
    tail = jnp.zeros((SLOTS, SIDE), jnp.int32)
    for s in range(SLOTS):
        owner = table[0, attr[0, s]]
        live = s < count[0, 0]
        tail = jnp.where(lane == s, jnp.where(live, decode(owner, core, u, v), 112), tail)
        sent = jnp.where(live, decode(owner, twin, twin_u, twin_v), 112)
        tail = jnp.where(lane == s + SLOTS, sent, tail)
        tail = jnp.where(lane == s + 2 * SLOTS, acct[0, s], tail)
    payload[TILES + ROWS :, :] = tail.astype(jnp.float32).astype(payload.dtype)
    prior.wait()
    for n in range(4):
        scale = column(lax.rsqrt(degree[n : n + 1, :].astype(jnp.float32)))
        scaled = rows[pl.ds(n * SIDE, SIDE), :].astype(jnp.float32) * scale
        payload[pl.ds(TILES + n * SIDE, SIDE), :] = scaled.astype(payload.dtype)
    tiles.wait()


def tile(sent, s):
    return sent[pl.ds(pl.multiple_of(s * SIDE, SIDE), SIDE), :]


def forward_kernel(offsets, tail0, tail1, sent0, sent1, *refs):
    outs, acc = refs[:-1], refs[-1]
    acc[...] = jnp.zeros_like(acc)
    for half, (tail, sent) in enumerate(((tail0, sent0), (tail1, sent1))):

        def step(s, carry, half=half, tail=tail, sent=sent):
            code, block = tail[0, half * SLOTS + s], tail[0, 2 * SLOTS + s]
            chip, along = code >> 4, code & 15
            index = jnp.int32(0)
            wanted = jnp.bool_(False)
            for n, offset in enumerate(offsets):
                index = jnp.where(chip == offset, n * LINE, index)
                wanted = wanted | (chip == offset)

            @pl.when(wanted)
            def _():
                acc[index + along] += lax.dot_general(
                    tile(sent, s),
                    tile(sent, SLOTS + block),
                    (((0,), (0,)), ((), ())),
                    preferred_element_type=jnp.float32,
                )

            return carry

        lax.fori_loop(0, SLOTS, step, 0, unroll=True)
    for n, out in enumerate(outs):
        out[...] = acc[n * LINE : (n + 1) * LINE].astype(out.dtype)


def near_kernel(me, parts, degree, sums):
    for n in range(4):
        total = parts[0, n].astype(jnp.float32)
        for k in range(1, 4):
            total += parts[k, n].astype(jnp.float32)
        sums[n * SIDE : (n + 1) * SIDE, :] = total.astype(sums.dtype)
    row = lax.broadcasted_iota(jnp.int32, (SLOTS, SIDE), 0)
    mine = jnp.where(row == where(me[0])[1] >> 2, degree[...].astype(jnp.float32), 0.0)
    sums[FOUR:, :] = mine.astype(sums.dtype)


def far_kernel(me, mine, other, own, spread):
    degree = mine[FOUR:, :].astype(jnp.float32) + other[FOUR:, :].astype(jnp.float32)
    for n in range(4):
        rows = pl.ds(n * SIDE, SIDE)
        total = mine[rows, :].astype(jnp.float32) + other[rows, :].astype(jnp.float32)
        scores = (total * column(lax.rsqrt(degree[n : n + 1, :]))).astype(spread.dtype)
        for k in range(4):
            spread[k, rows, :] = scores
    far = where(me[0])[1] >> 2
    own[...] = spread[0, pl.ds(pl.multiple_of(far * SIDE, SIDE), SIDE), :]


def backward_kernel(chips, halves, *refs):
    tails, sents, refs = refs[: len(halves)], refs[len(halves) : 2 * len(halves)], refs[2 * len(halves) :]
    groups, refs = refs[: len(chips)], refs[len(chips) :]
    if len(refs) == 1:
        (acc,) = refs
        acc[...] = jnp.zeros_like(acc)
        base = 0
    else:
        before, out, acc = refs
        base = halves[0] * ROWS
        acc[...] = before[base : base + ROWS, :]
    for half, tail, sent in zip(halves, tails, sents):

        def step(s, carry, half=half, tail=tail, sent=sent):
            code, block = tail[0, half * SLOTS + s], tail[0, 2 * SLOTS + s]
            chip, along = code >> 4, code & 15
            for n, blocks in zip(chips, groups):

                @pl.when(chip == n)
                def _(blocks=blocks):
                    start = pl.multiple_of(half * ROWS - base + block * SIDE, SIDE)
                    acc[pl.ds(start, SIDE), :] += jnp.dot(
                        tile(sent, s), tile(blocks, along), preferred_element_type=jnp.float32
                    )

            return carry

        lax.fori_loop(0, SLOTS, step, 0, unroll=True)
    if len(refs) > 1:
        out[...] = acc[...].astype(out.dtype)


def finish_kernel(types, scores, degree, seed, new):
    for n in range(4):
        rows = pl.ds(n * SIDE, SIDE)
        scale = column(lax.rsqrt(degree[n : n + 1, :].astype(jnp.float32)))
        prior = scores[rows, :].astype(jnp.float32)
        whole = types[0, rows, :].astype(jnp.float32)
        for k in range(1, 4):
            whole += types[k, rows, :].astype(jnp.float32)
        mixed = ALPHA * (whole * scale) + (1.0 - ALPHA) * prior
        kept = column(seed[n : n + 1, :].astype(jnp.float32))
        new[rows, :] = jnp.where(kept == 1.0, prior, mixed)


def smem(n):
    return [pl.BlockSpec(memory_space=pltpu.SMEM)] * n


def vmem(n):
    return [pl.BlockSpec(memory_space=pltpu.VMEM)] * n


def call(kernel, outs, specs, scratch, flops, moved):
    return pl.pallas_call(
        kernel,
        out_shape=outs,
        in_specs=specs,
        out_specs=vmem(len(outs)),
        scratch_shapes=scratch,
        compiler_params=pltpu.CompilerParams(vmem_limit_bytes=24 * MEBI),
        cost_estimate=pl.CostEstimate(flops=flops, bytes_accessed=moved, transcendentals=0),
    )


def per_device(
    scores0,
    seed_mask,
    acct_degree,
    attr_degree,
    tile_weight,
    tile_acct,
    tile_attr,
    attr_owner,
    tile_count,
):
    bf16, f32, i32 = jnp.bfloat16, jnp.float32, jnp.int32
    group = jax.ShapeDtypeStruct((LINE, SIDE, SIDE), bf16)
    degree = acct_degree.reshape(4, SIDE)
    me = lax.axis_index("acct").astype(i32).reshape(1)
    (payload,) = call(
        prepare_kernel,
        [jax.ShapeDtypeStruct((SENT, SIDE), bf16)],
        smem(2) + [pl.BlockSpec(memory_space=pltpu.HBM)] * 6,
        [
            pltpu.SMEM((1, SIDE), i32),
            pltpu.SMEM((1, SLOTS), i32),
            pltpu.SMEM((1, SLOTS), i32),
            pltpu.VMEM((ROWS, SIDE), bf16),
            pltpu.VMEM((4, SIDE), i32),
            pltpu.SemaphoreType.DMA((6,)),
        ],
        ROWS * SIDE,
        MEBI,
    )(
        me,
        tile_count,
        *(
            pltpu.with_memory_space_constraint(array, pltpu.HBM)
            for array in (
                attr_owner,
                tile_attr,
                tile_acct,
                tile_weight.reshape(TILES, SIDE),
                scores0,
                degree,
            )
        ),
    )
    payload1 = lax.ppermute(payload, "acct", SWAP)
    flops = 2 * 10 * SIDE**3
    tails = [sent[TILES + ROWS :][:1].astype(i32) for sent in (payload, payload1)]
    slots = (*tails, payload, payload1)

    def forward(chips):
        return call(
            functools.partial(forward_kernel, chips),
            [group] * len(chips),
            smem(2) + vmem(2),
            [pltpu.VMEM((len(chips) * LINE, SIDE, SIDE), f32)],
            flops,
            3 * MEBI,
        )(*slots)

    o3, o1, o2 = forward((3, 1, 2))
    r3 = lax.ppermute(o3, "acct", DIAGONAL)
    r1 = lax.ppermute(o1, "acct", BESIDE)
    r2 = lax.ppermute(o2, "acct", ACROSS)
    (o0,) = forward((0,))
    line = o0.astype(f32) + r1.astype(f32) + r2.astype(f32) + r3.astype(f32)
    line = line.astype(bf16).reshape(4, 4, SIDE, SIDE)
    line = lax.all_to_all(line, "acct", 0, 0, tiled=True, axis_index_groups=QUADS)
    sums = jax.ShapeDtypeStruct((FOUR + SLOTS, SIDE), bf16)
    (near,) = call(
        near_kernel, [sums], smem(1) + vmem(2), [], SIDE * SIDE * LINE, MEBI
    )(me, line, attr_degree)
    half = near.astype(f32) + lax.ppermute(near, "acct", FIRST).astype(f32)
    half = half.astype(bf16)
    rest = lax.ppermute(half, "acct", SECOND)
    own_scores, spread = call(
        far_kernel,
        [
            jax.ShapeDtypeStruct((SIDE, SIDE), bf16),
            jax.ShapeDtypeStruct((4, FOUR, SIDE), bf16),
        ],
        smem(1) + vmem(2),
        [],
        SIDE * SIDE * LINE,
        MEBI // 2,
    )(me, half, rest)

    g0 = lax.all_to_all(spread, "acct", 0, 0, tiled=True, axis_index_groups=QUADS)
    g0 = g0.reshape(LINE * SIDE, SIDE)
    g3 = lax.ppermute(g0, "acct", DIAGONAL)
    g1 = lax.ppermute(g0, "acct", BESIDE)
    g2 = lax.ppermute(g0, "acct", ACROSS)
    acc = jax.ShapeDtypeStruct((2 * ROWS, SIDE), f32)
    (before,) = call(
        functools.partial(backward_kernel, (0,), (0, 1)),
        [acc],
        smem(2) + vmem(3),
        [],
        flops,
        4 * MEBI,
    )(*slots, g0)

    def backward(half, dtype):
        (out,) = call(
            functools.partial(backward_kernel, (3, 1, 2), (half,)),
            [jax.ShapeDtypeStruct((ROWS, SIDE), dtype)],
            smem(1) + vmem(5),
            [pltpu.VMEM((ROWS, SIDE), f32)],
            flops,
            2 * MEBI,
        )(slots[half], slots[2 + half], g3, g1, g2, before)
        return out

    other = lax.ppermute(backward(1, bf16), "acct", SWAP)
    returned = (backward(0, f32) + other.astype(f32)).astype(bf16)
    types = jnp.broadcast_to(returned[None], (4, ROWS, SIDE))
    types = lax.all_to_all(types, "attr", 0, 0, tiled=True)
    (new_scores,) = call(
        finish_kernel,
        [jax.ShapeDtypeStruct((ROWS, SIDE), f32)],
        vmem(4),
        [],
        ROWS * SIDE * 8,
        MEBI,
    )(types, scores0, degree, seed_mask.reshape(4, SIDE))
    return (new_scores, own_scores[None])


def solution(mesh):
    placed = (
        P("acct", None),
        P("acct"),
        P("acct"),
        P("attr", "acct"),
        P("attr", "acct", None, None),
        P("attr", "acct"),
        P("attr", "acct"),
        P("attr", None),
        P("attr", "acct"),
    )
    return jax.shard_map(
        per_device,
        mesh=mesh,
        in_specs=placed,
        out_specs=(P("acct", None), P("attr", "acct", None)),
        check_vma=False,
    )
```

```python
import functools
import jax
import jax.numpy as jnp
from jax import lax
from jax.experimental import pallas as pl
from jax.experimental.pallas import tpu as pltpu
from jax.sharding import PartitionSpec as P

ALPHA = 0.8
SIDE = 128
SLOTS = 16
ROWS = 512
LINE = 16
MEBI = 2**20
TILES = SLOTS * SIDE
SENT = TILES + ROWS + SLOTS
FOUR = 4 * SIDE


def device(core, u, v):
    return (((u + core) % 16) * 4 + (v + core) % 4) * 2 + core


def pairs(meet):
    return [
        (device(c, u, v), device(c, *meet(c, u, v)))
        for c in range(2)
        for u in range(16)
        for v in range(4)
    ]


SWAP = [(i, i ^ 1) for i in range(128)]
BESIDE = pairs(lambda c, u, v: (u ^ 1, v))
ACROSS = pairs(lambda c, u, v: (u, v ^ 1))
DIAGONAL = pairs(lambda c, u, v: (u ^ 1, v ^ 1))
FIRST = pairs(lambda c, u, v: (u ^ 4 if c == 0 else 12 - (u & 12) + (u & 3), v))
SECOND = pairs(lambda c, u, v: (u ^ 4 if c == 1 else 12 - (u & 12) + (u & 3), v))
QUADS = [
    [device(c, far * 4 + step * 2 + odd, (0, 3, 1, 2)[side * 2 + end]) for end in (0, 1) for step in (0, 1)]
    for c in (0, 1)
    for side in (0, 1)
    for odd in (0, 1)
    for far in range(4)
]
def where(index):
    core = index & 1
    return core, ((index >> 3) - core) & 15, ((index >> 1) - core) & 3


def decode(owner, core, u, v):
    core1, u1, v1 = where(owner)
    side = (v ^ (v >> 1) ^ v1 ^ (v1 >> 1)) & 1
    chip = jnp.where(core1 == core, side * 2 + ((u ^ u1) & 1), 7)
    return chip * 16 + (v1 >> 1) * 8 + ((u1 >> 1) & 1) * 4 + (u1 >> 2)


def column(row):
    return jnp.broadcast_to(row, (SIDE, SIDE)).T


def prepare_kernel(me, table, attr, acct, count, weights, scores, degrees, payload, rows, degree, sems):
    tiles = pltpu.make_async_copy(weights, payload.at[pl.ds(0, TILES), :], sems.at[0])
    prior = pltpu.make_async_copy(scores, rows, sems.at[1])
    small = pltpu.make_async_copy(degrees, degree, sems.at[2])
    small.start()
    prior.start()
    tiles.start()
    core, u, v = where(me[0])
    twin, twin_u, twin_v = where(me[0] ^ 1)
    lane = lax.broadcasted_iota(jnp.int32, (SLOTS, SIDE), 1)
    tail = jnp.zeros((SLOTS, SIDE), jnp.int32)
    for s in range(SLOTS):
        owner = table[0, attr[0, s]]
        live = s < count[0, 0]
        tail = jnp.where(lane == s, jnp.where(live, decode(owner, core, u, v), 112), tail)
        sent = jnp.where(live, decode(owner, twin, twin_u, twin_v), 112)
        tail = jnp.where(lane == s + SLOTS, sent, tail)
        tail = jnp.where(lane == s + 2 * SLOTS, acct[0, s], tail)
    payload[TILES + ROWS :, :] = tail.astype(jnp.float32).astype(payload.dtype)
    small.wait()
    prior.wait()
    for n in range(4):
        scale = column(lax.rsqrt(degree[n : n + 1, :].astype(jnp.float32)))
        scaled = rows[pl.ds(n * SIDE, SIDE), :].astype(jnp.float32) * scale
        payload[pl.ds(TILES + n * SIDE, SIDE), :] = scaled.astype(payload.dtype)
    tiles.wait()


def tile(sent, s):
    return sent[pl.ds(pl.multiple_of(s * SIDE, SIDE), SIDE), :]


def forward_kernel(offsets, tail0, tail1, sent0, sent1, *refs):
    outs, acc = refs[:-1], refs[-1]
    acc[...] = jnp.zeros_like(acc)
    for half, (tail, sent) in enumerate(((tail0, sent0), (tail1, sent1))):

        def step(s, carry, half=half, tail=tail, sent=sent):
            code, block = tail[0, half * SLOTS + s], tail[0, 2 * SLOTS + s]
            chip, along = code >> 4, code & 15
            index = jnp.int32(0)
            wanted = jnp.bool_(False)
            for n, offset in enumerate(offsets):
                index = jnp.where(chip == offset, n * LINE, index)
                wanted = wanted | (chip == offset)

            @pl.when(wanted)
            def _():
                acc[index + along] += lax.dot_general(
                    tile(sent, s),
                    tile(sent, SLOTS + block),
                    (((0,), (0,)), ((), ())),
                    preferred_element_type=jnp.float32,
                )

            return carry

        lax.fori_loop(0, SLOTS, step, 0, unroll=True)
    for n, out in enumerate(outs):
        out[...] = acc[n * LINE : (n + 1) * LINE].astype(out.dtype)


def near_kernel(me, parts, degree, sums):
    for n in range(4):
        total = parts[0, n].astype(jnp.float32)
        for k in range(1, 4):
            total += parts[k, n].astype(jnp.float32)
        sums[n * SIDE : (n + 1) * SIDE, :] = total.astype(sums.dtype)
    row = lax.broadcasted_iota(jnp.int32, (SLOTS, SIDE), 0)
    mine = jnp.where(row == where(me[0])[1] >> 2, degree[...].astype(jnp.float32), 0.0)
    sums[FOUR:, :] = mine.astype(sums.dtype)


def far_kernel(me, mine, other, own, spread):
    degree = mine[FOUR:, :].astype(jnp.float32) + other[FOUR:, :].astype(jnp.float32)
    for n in range(4):
        rows = pl.ds(n * SIDE, SIDE)
        total = mine[rows, :].astype(jnp.float32) + other[rows, :].astype(jnp.float32)
        scores = (total * column(lax.rsqrt(degree[n : n + 1, :]))).astype(spread.dtype)
        for k in range(4):
            spread[k, rows, :] = scores
    far = where(me[0])[1] >> 2
    own[...] = spread[0, pl.ds(pl.multiple_of(far * SIDE, SIDE), SIDE), :]


def backward_kernel(chips, halves, *refs):
    tails, sents, refs = refs[: len(halves)], refs[len(halves) : 2 * len(halves)], refs[2 * len(halves) :]
    groups, refs = refs[: len(chips)], refs[len(chips) :]
    if len(refs) == 1:
        (acc,) = refs
        acc[...] = jnp.zeros_like(acc)
        base = 0
    else:
        before, out, acc = refs
        base = halves[0] * ROWS
        acc[...] = before[base : base + ROWS, :]
    for half, tail, sent in zip(halves, tails, sents):

        def step(s, carry, half=half, tail=tail, sent=sent):
            code, block = tail[0, half * SLOTS + s], tail[0, 2 * SLOTS + s]
            chip, along = code >> 4, code & 15
            for n, blocks in zip(chips, groups):

                @pl.when(chip == n)
                def _(blocks=blocks):
                    start = pl.multiple_of(half * ROWS - base + block * SIDE, SIDE)
                    acc[pl.ds(start, SIDE), :] += jnp.dot(
                        tile(sent, s), tile(blocks, along), preferred_element_type=jnp.float32
                    )

            return carry

        lax.fori_loop(0, SLOTS, step, 0, unroll=True)
    if len(refs) > 1:
        out[...] = acc[...].astype(out.dtype)


def finish_kernel(types, scores, degree, seed, new):
    for n in range(4):
        rows = pl.ds(n * SIDE, SIDE)
        scale = column(lax.rsqrt(degree[n : n + 1, :].astype(jnp.float32)))
        prior = scores[rows, :].astype(jnp.float32)
        whole = types[0, rows, :].astype(jnp.float32)
        for k in range(1, 4):
            whole += types[k, rows, :].astype(jnp.float32)
        mixed = ALPHA * (whole * scale) + (1.0 - ALPHA) * prior
        kept = column(seed[n : n + 1, :].astype(jnp.float32))
        new[rows, :] = jnp.where(kept == 1.0, prior, mixed)


def smem(n):
    return [pl.BlockSpec(memory_space=pltpu.SMEM)] * n


def vmem(n):
    return [pl.BlockSpec(memory_space=pltpu.VMEM)] * n


def call(kernel, outs, specs, scratch, flops, moved):
    return pl.pallas_call(
        kernel,
        out_shape=outs,
        in_specs=specs,
        out_specs=vmem(len(outs)),
        scratch_shapes=scratch,
        compiler_params=pltpu.CompilerParams(vmem_limit_bytes=24 * MEBI),
        cost_estimate=pl.CostEstimate(flops=flops, bytes_accessed=moved, transcendentals=0),
    )


def per_device(
    scores0,
    seed_mask,
    acct_degree,
    attr_degree,
    tile_weight,
    tile_acct,
    tile_attr,
    attr_owner,
    tile_count,
):
    bf16, f32, i32 = jnp.bfloat16, jnp.float32, jnp.int32
    group = jax.ShapeDtypeStruct((LINE, SIDE, SIDE), bf16)
    degree = acct_degree.reshape(4, SIDE)
    me = lax.axis_index("acct").astype(i32).reshape(1)
    (payload,) = call(
        prepare_kernel,
        [jax.ShapeDtypeStruct((SENT, SIDE), bf16)],
        smem(5) + [pl.BlockSpec(memory_space=pltpu.HBM)] * 3,
        [
            pltpu.VMEM((ROWS, SIDE), bf16),
            pltpu.VMEM((4, SIDE), i32),
            pltpu.SemaphoreType.DMA((3,)),
        ],
        ROWS * SIDE,
        MEBI,
    )(
        me,
        attr_owner,
        tile_attr,
        tile_acct,
        tile_count,
        *(
            pltpu.with_memory_space_constraint(array, pltpu.HBM)
            for array in (tile_weight.reshape(TILES, SIDE), scores0, degree)
        ),
    )
    payload1 = lax.ppermute(payload, "acct", SWAP)
    flops = 2 * 10 * SIDE**3
    tails = [sent[TILES + ROWS :][:1].astype(i32) for sent in (payload, payload1)]
    slots = (*tails, payload, payload1)

    def forward(chips):
        return call(
            functools.partial(forward_kernel, chips),
            [group] * len(chips),
            smem(2) + vmem(2),
            [pltpu.VMEM((len(chips) * LINE, SIDE, SIDE), f32)],
            flops,
            3 * MEBI,
        )(*slots)

    (o3,) = forward((3,))
    r3 = lax.ppermute(o3, "acct", DIAGONAL)
    o1, o2 = forward((1, 2))
    r1 = lax.ppermute(o1, "acct", BESIDE)
    r2 = lax.ppermute(o2, "acct", ACROSS)
    (o0,) = forward((0,))
    line = o0.astype(f32) + r1.astype(f32) + r2.astype(f32) + r3.astype(f32)
    line = line.astype(bf16).reshape(4, 4, SIDE, SIDE)
    line = lax.all_to_all(line, "acct", 0, 0, tiled=True, axis_index_groups=QUADS)
    sums = jax.ShapeDtypeStruct((FOUR + SLOTS, SIDE), bf16)
    (near,) = call(
        near_kernel, [sums], smem(1) + vmem(2), [], SIDE * SIDE * LINE, MEBI
    )(me, line, attr_degree)
    half = near.astype(f32) + lax.ppermute(near, "acct", FIRST).astype(f32)
    half = half.astype(bf16)
    rest = lax.ppermute(half, "acct", SECOND)
    own_scores, spread = call(
        far_kernel,
        [
            jax.ShapeDtypeStruct((SIDE, SIDE), bf16),
            jax.ShapeDtypeStruct((4, FOUR, SIDE), bf16),
        ],
        smem(1) + vmem(2),
        [],
        SIDE * SIDE * LINE,
        MEBI // 2,
    )(me, half, rest)

    g0 = lax.all_to_all(spread, "acct", 0, 0, tiled=True, axis_index_groups=QUADS)
    g0 = g0.reshape(LINE * SIDE, SIDE)
    g3 = lax.ppermute(g0, "acct", DIAGONAL)
    g1 = lax.ppermute(g0, "acct", BESIDE)
    g2 = lax.ppermute(g0, "acct", ACROSS)
    acc = jax.ShapeDtypeStruct((2 * ROWS, SIDE), f32)
    (before,) = call(
        functools.partial(backward_kernel, (0,), (0, 1)),
        [acc],
        smem(2) + vmem(3),
        [],
        flops,
        4 * MEBI,
    )(*slots, g0)

    def backward(half, dtype):
        (out,) = call(
            functools.partial(backward_kernel, (3, 1, 2), (half,)),
            [jax.ShapeDtypeStruct((ROWS, SIDE), dtype)],
            smem(1) + vmem(5),
            [pltpu.VMEM((ROWS, SIDE), f32)],
            flops,
            2 * MEBI,
        )(slots[half], slots[2 + half], g3, g1, g2, before)
        return out

    other = lax.ppermute(backward(1, bf16), "acct", SWAP)
    returned = (backward(0, f32) + other.astype(f32)).astype(bf16)
    types = jnp.broadcast_to(returned[None], (4, ROWS, SIDE))
    types = lax.all_to_all(types, "attr", 0, 0, tiled=True)
    (new_scores,) = call(
        finish_kernel,
        [jax.ShapeDtypeStruct((ROWS, SIDE), f32)],
        vmem(4),
        [],
        ROWS * SIDE * 8,
        MEBI,
    )(types, scores0, degree, seed_mask.reshape(4, SIDE))
    return (new_scores, own_scores[None])


def solution(mesh):
    placed = (
        P("acct", None),
        P("acct"),
        P("acct"),
        P("attr", "acct"),
        P("attr", "acct", None, None),
        P("attr", "acct"),
        P("attr", "acct"),
        P("attr", None),
        P("attr", "acct"),
    )
    return jax.shard_map(
        per_device,
        mesh=mesh,
        in_specs=placed,
        out_specs=(P("acct", None), P("attr", "acct", None)),
        check_vma=False,
    )
```
